32 devices in a mesh: dp: 4 (over z), tensor: 8 (over y, x, core).
Axes of the slice: x: 2, y: 2, z: 4, core: 2. Of those that a mesh axis runs over, the one named last changes fastest.
Arguments:
- acts: bfloat16 [4, 512, 4096], P('dp', None, 'tensor'), may hold values from -6 to 6
- grads: bfloat16 [4, 512, 4096], P('dp', None, 'tensor'), may hold values from -6 to 6
- basis_in_held: bfloat16 [4, 4096, 4096], P('dp', None, 'tensor'), may hold values from -0.09375 to 0.09375
- basis_out_held: bfloat16 [4, 4096, 4096], P('dp', None, 'tensor'), may hold values from -0.09375 to 0.09375
- owners: int32 [2, 8], replicated, may hold values from 0 to 3
- eig_lambda: bfloat16 [4096, 4096], P('tensor'), may hold values from 0.0049743652 to 0.19921875
Outputs:
- precond: bfloat16 [4, 4096, 4096], P('dp', 'tensor')
The draws below stay inside these ranges and needn't reach their ends.
Inputs may be any that keep to these rules, and one draw needn't show every extreme that they name: `owners`: row 0 is for the input eigenbasis, row 1 for the output eigenbasis; entry j names the dp group whose copy of column block j is current, the other copies of that block are stale.
All inputs are finite; a program needn't handle non-finite values.
Results may differ from the reference program's by a relative error of at most 0.0057.
Values may be sent and summed in bfloat16 or wider, within the bound.
No kernel may reach another device: no remote copies, remote signals or barrier semaphores. Data moves between devices by JAX's collectives and lax.ppermute only.
A program may use at most 64 MiB of HBM per device.

```python
import math
import jax
import jax.numpy as jnp
from jax import lax

D = 4096
TOK = 512
EXAMPLES = 4
N_DP = 4
N_TENSOR = 8


def with_ends(array, key, smallest, top_value):
    longest = array.shape.index(max(array.shape))
    spots = []
    for shift in (0, 1):
        where = [jax.random.randint(jax.random.fold_in(key, axis), (), 0, length) for axis, length in enumerate(array.shape)]
        where[longest] = (where[longest] + shift) % array.shape[longest]
        spots.append(tuple(where))
    return array.at[spots[0]].set(smallest).at[spots[1]].set(top_value)


def block_scale(own_key, shape, shards, smallest, largest):
    loudness = 1.0
    for axis_at, shards_of in shards:
        heights = jax.random.uniform(jax.random.fold_in(jax.random.fold_in(own_key, 6), axis_at), (shards_of,), jnp.float32, smallest / len(shards), largest / len(shards))
        loudness = loudness * jnp.repeat(jnp.exp(heights), shape[axis_at] // shards_of).reshape((-1,) + (1,) * (len(shape) - 1 - axis_at))
    return loudness


def scatter_about(own_key, shape, spread, most, cuts=(), kind=jnp.bfloat16):
    entries = spread * jax.random.normal(own_key, shape, jnp.float32)
    if cuts:
        entries = entries * block_scale(own_key, shape, cuts, -0.22, 0.18)
    return jnp.clip(entries, -most, most).astype(kind)


def setup_inputs(seed: int = 0) -> dict:
    streams_of = jax.random.split(jax.random.key(seed), 7)
    acts = scatter_about(streams_of[0], (EXAMPLES, TOK, D), 1.0, 6.0, ((0, 4), (2, 8)))
    grads = scatter_about(streams_of[1], (EXAMPLES, TOK, D), 1.0, 6.0, ((0, 4), (2, 8)))
    basis_in_held = scatter_about(streams_of[2], (EXAMPLES, D, D), D ** -0.5, 0.09375, ((0, 4), (2, 8)))
    basis_out_held = scatter_about(streams_of[3], (EXAMPLES, D, D), D ** -0.5, 0.09375, ((0, 4), (2, 8)))
    owners = with_ends(jax.random.randint(streams_of[4], (2, N_TENSOR), 0, N_DP), jax.random.fold_in(streams_of[4], 1), 0, N_DP - 1).astype(jnp.int32)
    eig_lambda = jnp.clip(jnp.exp(math.log(0.19921875) - 3.6901057 * jax.random.uniform(streams_of[5], (D, D), jnp.float32) ** block_scale(streams_of[5], (D, D), ((0, 8),), -0.2, 0.2)), 0.0049743652, 0.19921875).astype(jnp.bfloat16)
    return {"acts": acts, "grads": grads, "basis_in_held": basis_in_held, "basis_out_held": basis_out_held, "owners": owners, "eig_lambda": eig_lambda}


damping = 0.01


def assemble(held, picks):
    width = D // N_TENSOR
    blocks = held.reshape(N_DP, D, N_TENSOR, width)
    chosen = blocks[picks, :, jnp.arange(N_TENSOR, dtype=jnp.int32), :]
    return jnp.transpose(chosen, (1, 0, 2)).reshape(D, D)


def reference(acts, grads, basis_in_held, basis_out_held, owners, eig_lambda):
    basis_in = assemble(basis_in_held, owners[0])
    basis_out = assemble(basis_out_held, owners[1])
    denom = eig_lambda.astype(jnp.float32) + damping

    def one_example(pair):
        inputs, outputs = pair
        rot_in = jnp.dot(inputs, basis_in, preferred_element_type=jnp.float32).astype(jnp.bfloat16)
        rot_out = jnp.dot(outputs, basis_out, preferred_element_type=jnp.float32).astype(jnp.bfloat16)
        product = jnp.dot(rot_out.T, rot_in, preferred_element_type=jnp.float32) / TOK
        return (product / denom).astype(jnp.bfloat16)

    return lax.map(one_example, (acts, grads))
```

```python
import jax
import jax.numpy as jnp
from jax import lax
from jax.sharding import PartitionSpec as P

damping = 0.01
CHUNKS = 16
STREAMS = 2


def chain_broadcast(helds, owners, axis, n):
    me = lax.axis_index(axis)
    rows, cols = helds[0].shape
    size = rows // CHUNKS
    per = CHUNKS // STREAMS
    total = per * len(helds)
    outs = list(helds)

    def place(stream, c, k):
        return ((c - k * per) * STREAMS + stream) * size

    def own(stream, c, first, last):
        low, high = max(first, 0) // per, min(last, total - 1) // per
        picked = None
        for k in range(low, high + 1):
            at = place(stream, jnp.clip(c, k * per, (k + 1) * per - 1), k)
            block = lax.dynamic_slice(helds[k], (at, 0), (size, cols))
            picked = block if picked is None else jnp.where(c >= k * per, block, picked)
        return picked

    def owner_of(c):
        owner = owners[0]
        for k in range(1, len(helds)):
            owner = jnp.where(c >= k * per, owners[k], owner)
        return owner

    came = [[None, None] for _ in range(STREAMS)]
    sent = None
    for t in range(total + n - 2):
        for s in range(STREAMS):
            if came[s][0] is not None:
                came[s], _ = lax.optimization_barrier((came[s], sent))
            right = t - me
            left = t - (n - 1 - me)
            to_right = own(s, right, t - (n - 2), t)
            to_left = own(s, left, t - (n - 2), t)
            if came[s][0] is not None:
                to_right = jnp.where(owner_of(right) < me, came[s][0], to_right)
                to_left = jnp.where(owner_of(left) > me, came[s][1], to_left)
            live = [z for z in range(n - 1) if 0 <= t - z < total]
            from_left = lax.ppermute(to_right, axis, [(z, z + 1) for z in live])
            from_right = lax.ppermute(to_left, axis, [(n - 1 - z, n - 2 - z) for z in live])
            came[s] = [from_left, from_right]
            sent = [to_right, to_left]
            at_left, at_right = t - (me - 1), t - (n - 2 - me)
            first, last = max(t - (n - 2), 0), min(t, total - 1)
            for k in range(first // per, last // per + 1):
                behind = owners[k] < me
                c = jnp.where(behind, at_left, at_right)
                kept = jnp.clip(c, k * per, (k + 1) * per - 1)
                valid = (owners[k] != me) & (c == kept)
                at = place(s, kept, k)
                old = lax.dynamic_slice(outs[k], (at, 0), (size, cols))
                new = jnp.where(valid, jnp.where(behind, from_left, from_right), old)
                outs[k] = lax.dynamic_update_slice(outs[k], new, (at, 0))
    return outs


def shards(n_dp, acts, grads, basis_in_held, basis_out_held, owners, eig_lambda):
    column = lax.axis_index("tensor")
    all_acts = lax.all_gather(acts[0], "tensor", axis=1, tiled=True)
    all_grads = lax.all_gather(grads[0], "tensor", axis=1, tiled=True)
    basis_in, basis_out = chain_broadcast(
        [basis_in_held[0], basis_out_held[0]], [owners[0, column], owners[1, column]], "dp", n_dp
    )
    tokens = acts.shape[1]
    rot_in = jnp.dot(all_acts, basis_in, preferred_element_type=jnp.float32).astype(jnp.bfloat16)
    all_rot_in = lax.all_gather(rot_in, "tensor", axis=1, tiled=True)
    rot_out = jnp.dot(all_grads, basis_out, preferred_element_type=jnp.float32).astype(jnp.bfloat16)
    denom = eig_lambda.astype(jnp.float32) + damping
    contract = (((0,), (0,)), ((), ()))
    product = lax.dot_general(rot_out, all_rot_in, contract, preferred_element_type=jnp.float32) / tokens
    return (product / denom).astype(jnp.bfloat16)[None]


def solution(mesh):
    placed = (
        P("dp", None, "tensor"),
        P("dp", None, "tensor"),
        P("dp", None, "tensor"),
        P("dp", None, "tensor"),
        P(),
        P("tensor", None),
    )

    def step(*args):
        return shards(mesh.shape["dp"], *args)

    return jax.shard_map(step, mesh=mesh, in_specs=placed, out_specs=P("dp", "tensor", None), check_vma=False)
```

```python
import jax
import jax.numpy as jnp
from jax import lax
from jax.sharding import PartitionSpec as P

damping = 0.01
PARTS = 2


def from_owner(held, owner, n):
    rows = held.shape[0] // PARTS
    mine = lax.axis_index("dp") == owner
    out = []
    for part in range(PARTS):
        block = held[part * rows : (part + 1) * rows]
        block = jnp.where(mine, block, jnp.zeros_like(block))
        share = lax.psum_scatter(block, "dp", scatter_dimension=0, tiled=True)
        out.append(lax.all_gather(share, "dp", axis=0, tiled=True))
    return out


def rotate(rows, basis_parts):
    depth = basis_parts[0].shape[0]
    total = None
    for part, block in enumerate(basis_parts):
        term = jnp.dot(rows[:, part * depth : (part + 1) * depth], block, preferred_element_type=jnp.float32)
        total = term if total is None else total + term
    return total.astype(jnp.bfloat16)


def shards(n_dp, acts, grads, basis_in_held, basis_out_held, owners, eig_lambda):
    column = lax.axis_index("tensor")
    all_acts = lax.all_gather(acts[0], "tensor", axis=1, tiled=True)
    all_grads = lax.all_gather(grads[0], "tensor", axis=1, tiled=True)
    basis_in = from_owner(basis_in_held[0], owners[0, column], n_dp)
    basis_out = from_owner(basis_out_held[0], owners[1, column], n_dp)
    tokens = acts.shape[1]
    rot_in = rotate(all_acts, basis_in)
    all_rot_in = lax.all_gather(rot_in, "tensor", axis=1, tiled=True)
    rot_out = rotate(all_grads, basis_out)
    denom = eig_lambda.astype(jnp.float32) + damping
    contract = (((0,), (0,)), ((), ()))
    product = lax.dot_general(rot_out, all_rot_in, contract, preferred_element_type=jnp.float32) / tokens
    return (product / denom).astype(jnp.bfloat16)[None]


def solution(mesh):
    placed = (
        P("dp", None, "tensor"),
        P("dp", None, "tensor"),
        P("dp", None, "tensor"),
        P("dp", None, "tensor"),
        P(),
        P("tensor", None),
    )

    def step(*args):
        return shards(mesh.shape["dp"], *args)

    return jax.shard_map(step, mesh=mesh, in_specs=placed, out_specs=P("dp", "tensor", None), check_vma=False)
```

```python
import jax
import jax.numpy as jnp
from jax import lax
from jax.sharding import PartitionSpec as P

damping = 0.01
CHUNKS = 8
SHARE = 2


def summed(held, owner, axis):
    mine = lax.axis_index(axis) == owner
    return lax.psum(jnp.where(mine, held, jnp.zeros_like(held)), axis)


def chain_broadcast(helds, owners, first_row, axis, n):
    me = lax.axis_index(axis)
    rows, cols = helds[0].shape
    size = (rows - first_row) // CHUNKS
    per = CHUNKS
    total = per * len(helds)
    outs = [held[first_row:] for held in helds]

    def own(c, first, last):
        low, high = max(first, 0) // per, min(last, total - 1) // per
        picked = None
        for k in range(low, high + 1):
            at = first_row + jnp.clip(c - k * per, 0, per - 1) * size
            block = lax.dynamic_slice(helds[k], (at, 0), (size, cols))
            picked = block if picked is None else jnp.where(c >= k * per, block, picked)
        return picked

    def owner_of(c):
        owner = owners[0]
        for k in range(1, len(helds)):
            owner = jnp.where(c >= k * per, owners[k], owner)
        return owner

    came = None
    for t in range(total + n - 2):
        right = t - me
        left = t - (n - 1 - me)
        to_right = own(right, t - (n - 2), t)
        to_left = own(left, t - (n - 2), t)
        if came is not None:
            to_right = jnp.where(owner_of(right) < me, came[0], to_right)
            to_left = jnp.where(owner_of(left) > me, came[1], to_left)
        live = [z for z in range(n - 1) if 0 <= t - z < total]
        from_left = lax.ppermute(to_right, axis, [(z, z + 1) for z in live])
        from_right = lax.ppermute(to_left, axis, [(n - 1 - z, n - 2 - z) for z in live])
        came = [from_left, from_right]
        at_left, at_right = t - (me - 1), t - (n - 2 - me)
        first, last = max(t - (n - 2), 0), min(t, total - 1)
        for k in range(first // per, last // per + 1):
            behind = owners[k] < me
            c = jnp.where(behind, at_left, at_right) - k * per
            kept = jnp.clip(c, 0, per - 1)
            valid = (owners[k] != me) & (c == kept)
            at = kept * size
            old = lax.dynamic_slice(outs[k], (at, 0), (size, cols))
            new = jnp.where(valid, jnp.where(behind, from_left, from_right), old)
            outs[k] = lax.dynamic_update_slice(outs[k], new, (at, 0))
    return outs


def rotate(rows, parts):
    total, at = None, 0
    for block in parts:
        term = jnp.dot(rows[:, at : at + block.shape[0]], block, preferred_element_type=jnp.float32)
        total = term if total is None else total + term
        at += block.shape[0]
    return total.astype(jnp.bfloat16)


def shards(n_dp, acts, grads, basis_in_held, basis_out_held, owners, eig_lambda):
    column = lax.axis_index("tensor")
    owner_in, owner_out = owners[0, column], owners[1, column]
    held_in, held_out = basis_in_held[0], basis_out_held[0]
    split = held_in.shape[0] - held_in.shape[0] // SHARE
    all_acts = lax.all_gather(acts[0], "tensor", axis=1, tiled=True)
    all_grads = lax.all_gather(grads[0], "tensor", axis=1, tiled=True)
    top_in = summed(held_in[:split], owner_in, "dp")
    later, _ = lax.optimization_barrier((held_out[:split], top_in))
    top_out = summed(later, owner_out, "dp")
    low_in, low_out = chain_broadcast([held_in, held_out], [owner_in, owner_out], split, "dp", n_dp)
    tokens = acts.shape[1]
    rot_in = rotate(all_acts, [top_in, low_in])
    all_rot_in = lax.all_gather(rot_in, "tensor", axis=1, tiled=True)
    rot_out = rotate(all_grads, [top_out, low_out])
    denom = eig_lambda.astype(jnp.float32) + damping
    contract = (((0,), (0,)), ((), ()))
    product = lax.dot_general(rot_out, all_rot_in, contract, preferred_element_type=jnp.float32) / tokens
    return (product / denom).astype(jnp.bfloat16)[None]


def solution(mesh):
    placed = (
        P("dp", None, "tensor"),
        P("dp", None, "tensor"),
        P("dp", None, "tensor"),
        P("dp", None, "tensor"),
        P(),
        P("tensor", None),
    )

    def step(*args):
        return shards(mesh.shape["dp"], *args)

    return jax.shard_map(step, mesh=mesh, in_specs=placed, out_specs=P("dp", "tensor", None), check_vma=False)
```

```python
import jax
import jax.numpy as jnp
from jax import lax
from jax.sharding import PartitionSpec as P

damping = 0.01
ROOM = 2**24


def product_and_divide(rot_out, all_rot_in, eig_lambda, tokens):
    denom = eig_lambda.astype(jnp.float32) + damping
    contract = (((0,), (0,)), ((), ()))
    product = lax.dot_general(rot_out, all_rot_in, contract, preferred_element_type=jnp.float32) / tokens
    return (product / denom).astype(jnp.bfloat16)[None]


def from_owner(held, owner):
    return lax.psum(jnp.where(lax.axis_index("dp") == owner, held, jnp.zeros_like(held)), "dp")


def dot(a, b):
    return jnp.dot(a, b, preferred_element_type=jnp.float32)


def move_bases(acts, grads, basis_in_held, basis_out_held, owners, eig_lambda):
    column = lax.axis_index("tensor")
    basis_in = from_owner(basis_in_held[0], owners[0, column])
    basis_out = from_owner(basis_out_held[0], owners[1, column])
    rot_in = dot(lax.all_gather(acts[0], "tensor", axis=1, tiled=True), basis_in).astype(jnp.bfloat16)
    rot_out = dot(lax.all_gather(grads[0], "tensor", axis=1, tiled=True), basis_out).astype(jnp.bfloat16)
    return product_and_divide(
        rot_out, lax.all_gather(rot_in, "tensor", axis=1, tiled=True), eig_lambda, acts.shape[1]
    )


def swap(block, bit, n):
    return lax.ppermute(block, "tensor", [(j, j ^ bit) for j in range(n)])


def gather_plane(block, bits, n):
    width = block.shape[1]
    found = {0: block}
    for bit in bits:
        order = sorted(found)
        came = swap(jnp.concatenate([found[i] for i in order], axis=1), bit, n)
        for at, i in enumerate(order):
            found[i ^ bit] = came[:, at * width : (at + 1) * width]
    return jnp.concatenate([found[i] for i in sorted(found)], axis=1)


def in_order(held, column, n, keep=None):
    width = held.shape[0] // n
    offsets = list(range(0, n, 2)) + list(range(1, n, 2))
    blocks = [lax.dynamic_slice(held, ((column ^ i) * width, 0), (width, held.shape[1])) for i in offsets]
    if keep is not None:
        blocks = [jnp.where(keep, block, jnp.zeros_like(block)) for block in blocks]
    return jnp.concatenate(blocks, axis=0)


def move_inputs(n_dp, n, acts, grads, basis_in_held, basis_out_held, owners, eig_lambda):
    column = lax.axis_index("tensor")
    me = lax.axis_index("dp")
    owner_in, owner_out = owners[0, column], owners[1, column]
    half = basis_in_held.shape[1] // 2
    bits = []
    while 2 << len(bits) < n:
        bits.append(2 << len(bits))
    orders = (bits, bits[::-1])

    pieces = [acts[0]]
    for i in range(1, n_dp):
        pieces.append(lax.ppermute(acts[0], "dp", [(z, (z - i) % n_dp) for z in range(n_dp)]))

    masked_out = in_order(basis_out_held[0], column, n, me == owner_out)
    basis_out = lax.psum(masked_out, "dp")
    pieces = [lax.optimization_barrier((piece, masked_out))[0] for piece in pieces]
    own_grads, _ = lax.optimization_barrier((grads[0], masked_out))
    basis_in = in_order(basis_in_held[0], column, n)

    def rotate(even, odd, basis):
        return (dot(even, basis[:half]) + dot(odd, basis[half:])).astype(jnp.bfloat16)

    grads_even = gather_plane(own_grads, orders[1], n)
    grads_odd = swap(grads_even, 1, n)

    rot_in = None
    for i in range(n_dp):
        if i == n_dp - 1:
            tokens = acts.shape[1] // 2
            even = jnp.concatenate(
                [gather_plane(pieces[i][:tokens], orders[0], n), gather_plane(pieces[i][tokens:], orders[1], n)], axis=0
            )
        else:
            even = gather_plane(pieces[i], orders[0 if i == 0 else (i + 1) % 2], n)
        rot = rotate(even, swap(even, 1, n), basis_in)
        if i == 0:
            rot_in = rot
        else:
            rot = lax.ppermute(rot, "dp", [(z, (z + i) % n_dp) for z in range(n_dp)])
            rot_in = jnp.where((me - owner_in) % n_dp == i, rot, rot_in)

    all_rot_in = lax.all_gather(rot_in, "tensor", axis=1, tiled=True)
    rot_out = rotate(grads_even, grads_odd, basis_out)
    return product_and_divide(rot_out, all_rot_in, eig_lambda, acts.shape[1])


def solution(mesh):
    placed = (
        P("dp", None, "tensor"),
        P("dp", None, "tensor"),
        P("dp", None, "tensor"),
        P("dp", None, "tensor"),
        P(),
        P("tensor", None),
    )
    n_dp, n_tensor = mesh.shape["dp"], mesh.shape["tensor"]

    def step(acts, *rest):
        whole = n_dp * acts.shape[1] * acts.shape[2] * n_tensor * acts.dtype.itemsize
        if whole <= ROOM and n_tensor & (n_tensor - 1) == 0:
            return move_inputs(n_dp, n_tensor, acts, *rest)
        return move_bases(acts, *rest)

    return jax.shard_map(step, mesh=mesh, in_specs=placed, out_specs=P("dp", "tensor", None), check_vma=False)
```

```python
import jax
import jax.numpy as jnp
from jax import lax
from jax.sharding import PartitionSpec as P

damping = 0.01
ROOM = 2**25


def product_and_divide(rot_out, all_rot_in, eig_lambda, tokens):
    denom = eig_lambda.astype(jnp.float32) + damping
    contract = (((0,), (0,)), ((), ()))
    product = lax.dot_general(rot_out, all_rot_in, contract, preferred_element_type=jnp.float32) / tokens
    return (product / denom).astype(jnp.bfloat16)[None]


def from_owner(held, owner):
    return lax.psum(jnp.where(lax.axis_index("dp") == owner, held, jnp.zeros_like(held)), "dp")


def dot(a, b):
    return jnp.dot(a, b, preferred_element_type=jnp.float32)


def move_bases(acts, grads, basis_in_held, basis_out_held, owners, eig_lambda):
    column = lax.axis_index("tensor")
    basis_in = from_owner(basis_in_held[0], owners[0, column])
    basis_out = from_owner(basis_out_held[0], owners[1, column])
    rot_in = dot(lax.all_gather(acts[0], "tensor", axis=1, tiled=True), basis_in).astype(jnp.bfloat16)
    rot_out = dot(lax.all_gather(grads[0], "tensor", axis=1, tiled=True), basis_out).astype(jnp.bfloat16)
    return product_and_divide(
        rot_out, lax.all_gather(rot_in, "tensor", axis=1, tiled=True), eig_lambda, acts.shape[1]
    )


def swap(block, bit, n):
    return lax.ppermute(block, "tensor", [(j, j ^ bit) for j in range(n)])


def side_by_side(found):
    return jnp.concatenate([found[i] for i in sorted(found)], axis=1)


def exchange(found, bit, n):
    order = sorted(found)
    came = swap(side_by_side(found), bit, n)
    width = came.shape[1] // len(order)
    return found | {i ^ bit: came[:, at * width : (at + 1) * width] for at, i in enumerate(order)}


def in_order(held, column, n):
    width = held.shape[0] // n
    offsets = list(range(0, n, 2)) + list(range(1, n, 2))
    blocks = [lax.dynamic_slice(held, ((column ^ i) * width, 0), (width, held.shape[1])) for i in offsets]
    return jnp.concatenate(blocks, axis=0)


def after(value, *others):
    return lax.optimization_barrier((value, *others))[0]


def move_inputs(n_dp, n, acts, grads, basis_in_held, basis_out_held, owners, eig_lambda):
    column = lax.axis_index("tensor")
    me = lax.axis_index("dp")
    mine = (acts[0], grads[0])
    held = (basis_in_held[0], basis_out_held[0])
    behind = [(me - owners[side, column]) % n_dp for side in (0, 1)]
    half = held[0].shape[0] // 2
    bits = []
    while 2 << len(bits) < n:
        bits.append(2 << len(bits))

    keys = [(side, i) for side in (0, 1) for i in range(1, n_dp)]
    pieces = {(side, i): lax.ppermute(mine[side], "dp", [(z, (z - i) % n_dp) for z in range(n_dp)]) for side, i in keys}
    gathered = [lax.all_gather(block, "tensor", axis=1, tiled=True) for block in mine]
    ordered = [in_order(block, column, n) for block in held]
    rotated = [dot(gathered[side], held[side]).astype(jnp.bfloat16) for side in (0, 1)]

    def finish(key, found):
        side, i = key
        even = side_by_side(found)
        odd = swap(even, 1, n)
        rot = (dot(even, ordered[side][:half]) + dot(odd, ordered[side][half:])).astype(jnp.bfloat16)
        rot = lax.ppermute(rot, "dp", [(z, (z + i) % n_dp) for z in range(n_dp)])
        rotated[side] = jnp.where(behind[side] == i, rot, rotated[side])

    last = None
    for at in range(0, len(keys), 2):
        pair = keys[at : at + 2]
        found = [{0: pieces[key]} for key in pair]
        for level in range(len(bits)):
            if last is not None:
                found = after(found, last)
            last = found
            found = [exchange(f, (bits, bits[::-1])[p][level], n) for p, f in enumerate(found)]
        for key, f in zip(pair, found):
            finish(key, f)

    rot_in, rot_out = rotated
    all_rot_in = lax.all_gather(rot_in, "tensor", axis=1, tiled=True)
    return product_and_divide(rot_out, all_rot_in, eig_lambda, acts.shape[1])


def solution(mesh):
    placed = (
        P("dp", None, "tensor"),
        P("dp", None, "tensor"),
        P("dp", None, "tensor"),
        P("dp", None, "tensor"),
        P(),
        P("tensor", None),
    )
    n_dp, n_tensor = mesh.shape["dp"], mesh.shape["tensor"]

    def step(acts, *rest):
        whole = 2 * n_dp * acts.shape[1] * acts.shape[2] * n_tensor * acts.dtype.itemsize
        if whole <= ROOM and n_tensor & (n_tensor - 1) == 0:
            return move_inputs(n_dp, n_tensor, acts, *rest)
        return move_bases(acts, *rest)

    return jax.shard_map(step, mesh=mesh, in_specs=placed, out_specs=P("dp", "tensor", None), check_vma=False)
```

```python
import jax
import jax.numpy as jnp
from jax import lax
from jax.sharding import PartitionSpec as P

damping = 0.01
ROOM = 2**25


def product_and_divide(rot_out, all_rot_in, eig_lambda, tokens):
    denom = eig_lambda.astype(jnp.float32) + damping
    contract = (((0,), (0,)), ((), ()))
    product = lax.dot_general(rot_out, all_rot_in, contract, preferred_element_type=jnp.float32) / tokens
    return (product / denom).astype(jnp.bfloat16)[None]


def from_owner(held, owner):
    return lax.psum(jnp.where(lax.axis_index("dp") == owner, held, jnp.zeros_like(held)), "dp")


def dot(a, b):
    return jnp.dot(a, b, preferred_element_type=jnp.float32)


def move_bases(acts, grads, basis_in_held, basis_out_held, owners, eig_lambda):
    column = lax.axis_index("tensor")
    basis_in = from_owner(basis_in_held[0], owners[0, column])
    basis_out = from_owner(basis_out_held[0], owners[1, column])
    rot_in = dot(lax.all_gather(acts[0], "tensor", axis=1, tiled=True), basis_in).astype(jnp.bfloat16)
    rot_out = dot(lax.all_gather(grads[0], "tensor", axis=1, tiled=True), basis_out).astype(jnp.bfloat16)
    return product_and_divide(
        rot_out, lax.all_gather(rot_in, "tensor", axis=1, tiled=True), eig_lambda, acts.shape[1]
    )


X, Y, CORE = 2, 4, 1


def swap(block, bit):
    return lax.ppermute(block, "tensor", [(j, j ^ bit) for j in range(X + Y + CORE + 1)])


def in_order(held, column):
    width = held.shape[0] // (X + Y + CORE + 1)
    offsets = [0, X, Y, X + Y]
    offsets += [CORE + i for i in offsets]
    blocks = [lax.dynamic_slice(held, ((column ^ i) * width, 0), (width, held.shape[1])) for i in offsets]
    return jnp.concatenate(blocks, axis=0)


def after(values, *others):
    return lax.optimization_barrier((values, others))[0]


def move_inputs(n_dp, acts, grads, basis_in_held, basis_out_held, owners, eig_lambda):
    column = lax.axis_index("tensor")
    me = lax.axis_index("dp")
    mine = (acts[0], grads[0])
    held = (basis_in_held[0], basis_out_held[0])
    behind = [(me - owners[side, column]) % n_dp for side in (0, 1)]
    half = held[0].shape[0] // 2
    everyone = [lax.all_gather(block, "dp") for block in mine]
    ordered = [in_order(block, column) for block in held]

    def piece(side, i):
        if i == 0:
            return mine[side]
        return lax.dynamic_index_in_dim(everyone[side], (me + i) % n_dp, 0, keepdims=False)

    rotated, returned = {}, {}

    def rotate(key, blocks):
        side, i = key
        even = jnp.concatenate(blocks, axis=1)
        odd = swap(even, CORE)
        rotated[key] = (dot(even, ordered[side][:half]) + dot(odd, ordered[side][half:])).astype(jnp.bfloat16)
        returned[key] = rotated[key]
        if i:
            returned[key] = lax.ppermute(rotated[key], "dp", [(z, (z + i) % n_dp) for z in range(n_dp)])

    keys = [(0, 0), (1, 0)] + [(0, i) for i in range(1, n_dp)]
    keys += [(1, i) for i in sorted(range(1, n_dp), key=lambda i: -min(i, n_dp - i))]
    slots = []

    def slot(to_x, to_y):
        if slots:
            others = [slots[-1][0]]
            if len(slots) > 1:
                others.append(slots[-2][1])
            at = len(slots) // 3
            if at > 1 and len(slots) % 3 == 2:
                others.append([rotated[key] for key in keys[2 * at - 4 : 2 * at - 2]])
            if at > 2 and len(slots) % 3 == 2:
                others.append([returned[key] for key in keys[2 * at - 6 : 2 * at - 4]])
            to_x, to_y = after([to_x, to_y], *others)
        slots.append(([to_x, to_y], [swap(to_x, X), swap(to_y, Y)]))
        return slots[-1][1]

    for at in range(0, len(keys), 2):
        p, q = piece(*keys[at]), piece(*keys[at + 1])
        p_x, q_y = slot(p, q)
        q_x, p_y = slot(q, p)
        q_xy, p_xy = slot(q_y, p_x)
        rotate(keys[at], [p, p_x, p_y, p_xy])
        rotate(keys[at + 1], [q, q_x, q_y, q_xy])

    found = []
    for side in (0, 1):
        total = returned[side, 0]
        for i in range(1, n_dp):
            total = jnp.where(behind[side] == i, returned[side, i], total)
        found.append(total)
    all_rot_in = lax.all_gather(found[0], "tensor", axis=1, tiled=True)
    return product_and_divide(found[1], all_rot_in, eig_lambda, acts.shape[1])


def solution(mesh):
    placed = (
        P("dp", None, "tensor"),
        P("dp", None, "tensor"),
        P("dp", None, "tensor"),
        P("dp", None, "tensor"),
        P(),
        P("tensor", None),
    )
    n_dp, n_tensor = mesh.shape["dp"], mesh.shape["tensor"]

    def step(acts, *rest):
        whole = 2 * n_dp * acts.shape[1] * acts.shape[2] * n_tensor * acts.dtype.itemsize
        if whole <= ROOM and n_tensor == X + Y + CORE + 1:
            return move_inputs(n_dp, acts, *rest)
        return move_bases(acts, *rest)

    return jax.shard_map(step, mesh=mesh, in_specs=placed, out_specs=P("dp", "tensor", None), check_vma=False)
```

```python
import jax
import jax.numpy as jnp
from jax import lax
from jax.sharding import PartitionSpec as P

damping = 0.01
ROOM = 2**25


def product_and_divide(rot_out, all_rot_in, eig_lambda, tokens):
    denom = eig_lambda.astype(jnp.float32) + damping
    contract = (((0,), (0,)), ((), ()))
    product = lax.dot_general(rot_out, all_rot_in, contract, preferred_element_type=jnp.float32) / tokens
    return (product / denom).astype(jnp.bfloat16)[None]


def from_owner(held, owner):
    return lax.psum(jnp.where(lax.axis_index("dp") == owner, held, jnp.zeros_like(held)), "dp")


def dot(a, b):
    return jnp.dot(a, b, preferred_element_type=jnp.float32)


def move_bases(acts, grads, basis_in_held, basis_out_held, owners, eig_lambda):
    column = lax.axis_index("tensor")
    basis_in = from_owner(basis_in_held[0], owners[0, column])
    basis_out = from_owner(basis_out_held[0], owners[1, column])
    rot_in = dot(lax.all_gather(acts[0], "tensor", axis=1, tiled=True), basis_in).astype(jnp.bfloat16)
    rot_out = dot(lax.all_gather(grads[0], "tensor", axis=1, tiled=True), basis_out).astype(jnp.bfloat16)
    return product_and_divide(
        rot_out, lax.all_gather(rot_in, "tensor", axis=1, tiled=True), eig_lambda, acts.shape[1]
    )


X, Y, CORE = 2, 4, 1


def swap(block, bit):
    return lax.ppermute(block, "tensor", [(j, j ^ bit) for j in range(X + Y + CORE + 1)])


def shift(block, by, n):
    return lax.ppermute(block, "dp", [(z, (z + by) % n) for z in range(n)])


def in_order(held, column):
    width = held.shape[0] // (X + Y + CORE + 1)
    offsets = [0, X, Y, X + Y]
    offsets += [CORE + i for i in offsets]
    blocks = [lax.dynamic_slice(held, ((column ^ i) * width, 0), (width, held.shape[1])) for i in offsets]
    return jnp.concatenate(blocks, axis=0)


def after(values, others):
    return lax.optimization_barrier((values, others))[0]


def move_inputs(n_dp, acts, grads, basis_in_held, basis_out_held, owners, eig_lambda):
    column = lax.axis_index("tensor")
    me = lax.axis_index("dp")
    mine = (acts[0], grads[0])
    tokens = acts.shape[1]
    behind = [(me - owners[side, column]) % n_dp for side in (0, 1)]
    ordered = [in_order(block[0], column) for block in (basis_in_held, basis_out_held)]
    half = ordered[0].shape[0] // 2

    def near(i):
        return min(i, n_dp - i)

    acts_order = sorted(range(1, n_dp), key=near)
    grads_order = sorted(range(n_dp), key=lambda i: (-near(i), -i))
    groups = [[(0, 0)]]
    groups += [[(0, i) for i in acts_order[at : at + 2]] for at in range(0, len(acts_order), 2)]
    groups += [[(1, i) for i in grads_order[at : at + 2]] for at in range(0, len(grads_order), 2)]

    all_grads = lax.all_gather(mine[1], "dp")
    pieces = {(0, 0): mine[0], (1, 0): mine[1]}
    for i in acts_order[:2]:
        pieces[0, i] = shift(mine[0], -i, n_dp)
    for i in range(1, n_dp):
        pieces[1, i] = lax.dynamic_index_in_dim(all_grads, (me + i) % n_dp, 0, keepdims=False)

    due = []
    rotated, returned = {}, {}
    even = odd = None

    def rotate(group):
        side = group[0][0]
        low, high = ordered[side][:half], ordered[side][half:]
        rot = [(dot(e, low) + dot(o, high)).astype(jnp.bfloat16) for e, o in zip(even, odd)]
        if len(group) == 1:
            rotated[group[0]] = jnp.concatenate(rot, axis=0)
        else:
            rotated.update(zip(group, rot))
        return [rotated[key] for key in group]

    def send_back(group):
        for side, i in group:
            returned[side, i] = shift(rotated[side, i], i, n_dp) if i else rotated[side, i]

    for at, group in enumerate(groups):
        stack = jnp.concatenate([pieces[key] for key in group], axis=0)
        stack = after(stack, due)
        x, y = swap(stack, X), swap(stack, Y)
        due = [x, y]
        if at == 1:
            for i in acts_order[2:]:
                pieces[0, i] = shift(after(mine[0], stack), -i, n_dp)
        if at > 0:
            odd = [swap(block, CORE) for block in even]
            due.append(odd)
        if at > 1:
            send_back(groups[at - 2])
            due.append([returned[key] for key in groups[at - 2]])
        if at == 0:
            due.append([pieces[0, i] for i in acts_order[:2]])
        rows = stack.shape[0] // 2
        to_x, to_y = after((y[rows:], x[:rows]), due)
        diagonal = [swap(to_y, Y), swap(to_x, X)]
        due = [diagonal]
        if at > 0:
            due.append(rotate(groups[at - 1]))
        if at == 1:
            due.append([pieces[0, i] for i in acts_order[2:]])
        upper = jnp.concatenate([stack[:rows], x[:rows], y[:rows], diagonal[0]], axis=1)
        lower = jnp.concatenate([stack[rows:], x[rows:], y[rows:], diagonal[1]], axis=1)
        even = [upper, lower]

    send_back(groups[-2])
    even = after(even, due)
    odd = [swap(block, CORE) for block in even]
    rotate(groups[-1])
    send_back(groups[-1])

    found = []
    for side in (0, 1):
        total = returned[side, 0]
        for i in range(1, n_dp):
            total = jnp.where(behind[side] == i, returned[side, i], total)
        found.append(total)
    all_rot_in = lax.all_gather(found[0], "tensor", axis=1, tiled=True)
    return product_and_divide(found[1], all_rot_in, eig_lambda, tokens)


def solution(mesh):
    placed = (
        P("dp", None, "tensor"),
        P("dp", None, "tensor"),
        P("dp", None, "tensor"),
        P("dp", None, "tensor"),
        P(),
        P("tensor", None),
    )
    n_dp, n_tensor = mesh.shape["dp"], mesh.shape["tensor"]

    def step(acts, *rest):
        whole = 2 * n_dp * acts.shape[1] * acts.shape[2] * n_tensor * acts.dtype.itemsize
        if whole <= ROOM and n_tensor == X + Y + CORE + 1:
            return move_inputs(n_dp, acts, *rest)
        return move_bases(acts, *rest)

    return jax.shard_map(step, mesh=mesh, in_specs=placed, out_specs=P("dp", "tensor", None), check_vma=False)
```

```python
import jax
import jax.numpy as jnp
from jax import lax
from jax.sharding import PartitionSpec as P

damping = 0.01
ROOM = 2**25


def product_and_divide(rot_out, all_rot_in, eig_lambda, tokens):
    denom = eig_lambda.astype(jnp.float32) + damping
    contract = (((0,), (0,)), ((), ()))
    product = lax.dot_general(rot_out, all_rot_in, contract, preferred_element_type=jnp.float32) / tokens
    return (product / denom).astype(jnp.bfloat16)[None]


def from_owner(held, owner):
    return lax.psum(jnp.where(lax.axis_index("dp") == owner, held, jnp.zeros_like(held)), "dp")


def dot(a, b):
    return jnp.dot(a, b, preferred_element_type=jnp.float32)


def move_bases(acts, grads, basis_in_held, basis_out_held, owners, eig_lambda):
    column = lax.axis_index("tensor")
    basis_in = from_owner(basis_in_held[0], owners[0, column])
    basis_out = from_owner(basis_out_held[0], owners[1, column])
    rot_in = dot(lax.all_gather(acts[0], "tensor", axis=1, tiled=True), basis_in).astype(jnp.bfloat16)
    rot_out = dot(lax.all_gather(grads[0], "tensor", axis=1, tiled=True), basis_out).astype(jnp.bfloat16)
    return product_and_divide(
        rot_out, lax.all_gather(rot_in, "tensor", axis=1, tiled=True), eig_lambda, acts.shape[1]
    )


X, Y, CORE = 2, 4, 1


def swap(block, bit):
    return lax.ppermute(block, "tensor", [(j, j ^ bit) for j in range(X + Y + CORE + 1)])


def shift(block, by, n):
    return lax.ppermute(block, "dp", [(z, (z + by) % n) for z in range(n)])


def in_order(held, column):
    width = held.shape[0] // (X + Y + CORE + 1)
    offsets = [0, X, Y, X + Y]
    offsets += [CORE + i for i in offsets]
    blocks = [lax.dynamic_slice(held, ((column ^ i) * width, 0), (width, held.shape[1])) for i in offsets]
    return jnp.concatenate(blocks, axis=0)


def after(values, others):
    return lax.optimization_barrier((values, others))[0]


def move_inputs(n_dp, acts, grads, basis_in_held, basis_out_held, owners, eig_lambda):
    column = lax.axis_index("tensor")
    me = lax.axis_index("dp")
    mine = (acts[0], grads[0])
    tokens = acts.shape[1]
    behind = [(me - owners[side, column]) % n_dp for side in (0, 1)]
    ordered = [in_order(block[0], column) for block in (basis_in_held, basis_out_held)]
    half = ordered[0].shape[0] // 2

    def near(i):
        return min(i, n_dp - i)

    acts_order = sorted(range(1, n_dp), key=near)
    grads_order = sorted(range(1, n_dp), key=lambda i: (-near(i), -i))
    groups = [[(0, 0)]]
    groups += [[(0, i) for i in acts_order[at : at + 2]] for at in range(0, len(acts_order), 2)]
    groups += [[(1, i) for i in grads_order[at : at + 2]] for at in range(0, len(grads_order), 2)]
    groups += [[(1, 0)]]

    pieces = {(0, 0): mine[0], (1, 0): mine[1]}
    for i in acts_order[:2]:
        pieces[0, i] = shift(mine[0], -i, n_dp)

    due = []
    even = odd = None
    rotated, returned, over = {}, {}, set()

    def rotate(group):
        side = group[0][0]
        low, high = ordered[side][:half], ordered[side][half:]
        rot = [(dot(e, low) + dot(o, high)).astype(jnp.bfloat16) for e, o in zip(even, odd)]
        rotated.update(zip(group, rot))
        return rot

    def send_back(group):
        for side, i in group:
            returned[side, i] = shift(after(rotated[side, i], due), i, n_dp) if i else rotated[side, i]

    for at, group in enumerate(groups):
        before = groups[at - 1] if at else []
        stack = jnp.concatenate([pieces[key] for key in group], axis=0)
        stack = after(stack, due)
        if at == 1:
            for i in acts_order[2:]:
                pieces[0, i] = shift(after(mine[0], due), -i, n_dp)
            all_grads = lax.all_gather(after(mine[1], due), "dp")
            for i in range(1, n_dp):
                pieces[1, i] = lax.dynamic_index_in_dim(all_grads, (me + i) % n_dp, 0, keepdims=False)
        late = [key for key in rotated if key not in returned]
        send_back(late)
        x, y = swap(stack, X), swap(stack, Y)
        due = [x, y, [returned[key] for key in returned if key not in over and key[0] == 0]]
        over = set(returned)
        if at:
            odd = [swap(block, CORE) for block in even]
        early = len(group) >= len(before) and at > 1
        if early:
            due.append(rotate(before))
        rows = stack.shape[0] // 2
        to_x, to_y = after((y[rows:], x[:rows]), due)
        if early:
            send_back(before)
        diagonal = [swap(to_y, Y), swap(to_x, X)]
        due = [diagonal]
        if at and not early:
            due.append(rotate(before))
        if at < 2:
            due.append([pieces[0, i] for i in (acts_order[2:] if at else acts_order[:2])])
        if len(group) == 1:
            even = [jnp.concatenate([stack, x, y, after(jnp.concatenate(diagonal, axis=0), [])], axis=1)]
        else:
            even = [
                jnp.concatenate([stack[:rows], x[:rows], y[:rows], diagonal[0]], axis=1),
                jnp.concatenate([stack[rows:], x[rows:], y[rows:], diagonal[1]], axis=1),
            ]

    even = after(even, due)
    odd = [swap(block, CORE) for block in even]
    rotate(groups[-1])
    due = []
    send_back(groups[-1])

    found = []
    for side in (0, 1):
        total = returned[side, 0]
        for i in range(1, n_dp):
            total = jnp.where(behind[side] == i, returned[side, i], total)
        found.append(total)
    all_rot_in = lax.all_gather(found[0], "tensor", axis=1, tiled=True)
    return product_and_divide(found[1], all_rot_in, eig_lambda, tokens)


def solution(mesh):
    placed = (
        P("dp", None, "tensor"),
        P("dp", None, "tensor"),
        P("dp", None, "tensor"),
        P("dp", None, "tensor"),
        P(),
        P("tensor", None),
    )
    n_dp, n_tensor = mesh.shape["dp"], mesh.shape["tensor"]

    def step(acts, *rest):
        whole = 2 * n_dp * acts.shape[1] * acts.shape[2] * n_tensor * acts.dtype.itemsize
        if whole <= ROOM and n_tensor == X + Y + CORE + 1:
            return move_inputs(n_dp, acts, *rest)
        return move_bases(acts, *rest)

    return jax.shard_map(step, mesh=mesh, in_specs=placed, out_specs=P("dp", "tensor", None), check_vma=False)
```

```python
import jax
import jax.numpy as jnp
from jax import lax
from jax.sharding import PartitionSpec as P

damping = 0.01
ROOM = 2**25


def product_and_divide(rot_out, all_rot_in, eig_lambda, tokens):
    denom = eig_lambda.astype(jnp.float32) + damping
    contract = (((0,), (0,)), ((), ()))
    product = lax.dot_general(rot_out, all_rot_in, contract, preferred_element_type=jnp.float32) / tokens
    return (product / denom).astype(jnp.bfloat16)[None]


def from_owner(held, owner):
    return lax.psum(jnp.where(lax.axis_index("dp") == owner, held, jnp.zeros_like(held)), "dp")


def dot(a, b):
    return jnp.dot(a, b, preferred_element_type=jnp.float32)


def move_bases(acts, grads, basis_in_held, basis_out_held, owners, eig_lambda):
    column = lax.axis_index("tensor")
    basis_in = from_owner(basis_in_held[0], owners[0, column])
    basis_out = from_owner(basis_out_held[0], owners[1, column])
    rot_in = dot(lax.all_gather(acts[0], "tensor", axis=1, tiled=True), basis_in).astype(jnp.bfloat16)
    rot_out = dot(lax.all_gather(grads[0], "tensor", axis=1, tiled=True), basis_out).astype(jnp.bfloat16)
    return product_and_divide(
        rot_out, lax.all_gather(rot_in, "tensor", axis=1, tiled=True), eig_lambda, acts.shape[1]
    )


X, Y, CORE = 2, 4, 1


def swap(block, bit):
    return lax.ppermute(block, "tensor", [(j, j ^ bit) for j in range(X + Y + CORE + 1)])


def shift(block, by, n):
    return lax.ppermute(block, "dp", [(z, (z + by) % n) for z in range(n)])


def in_order(held, column, offsets):
    width = held.shape[0] // (X + Y + CORE + 1)
    blocks = [lax.dynamic_slice(held, ((column ^ i) * width, 0), (width, held.shape[1])) for i in offsets]
    return jnp.concatenate(blocks, axis=0)


def after(values, others):
    return lax.optimization_barrier((values, others))[0]


def move_inputs(n_dp, acts, grads, basis_in_held, basis_out_held, owners, eig_lambda):
    column = lax.axis_index("tensor")
    me = lax.axis_index("dp")
    own = (acts[0], grads[0])
    tokens = acts.shape[1]
    behind = [(me - owners[side, column]) % n_dp for side in (0, 1)]
    found = [0, X, Y, X + Y]
    held = (basis_in_held[0], basis_out_held[0])
    theirs = [swap(in_order(block, column, [CORE + i for i in found]), CORE) for block in held]
    ours = [in_order(block, column, found) for block in held]

    pieces = {(0, 0): own[0], (1, 0): own[1]}
    rotated, returned = {}, {}

    def fetch(key, gate):
        side, i = key
        pieces[key] = shift(after(own[side], gate), -i, n_dp)
        return pieces[key]

    def send_back(key, gate):
        side, i = key
        returned[key] = shift(after(rotated[key], gate), i, n_dp)
        return returned[key]

    def rotate(group, evens):
        crossing = [swap(dot(even, theirs[side]), CORE) for (side, _), even in zip(group, evens)]
        for (side, i), even, other in zip(group, evens, crossing):
            rotated[side, i] = (dot(even, ours[side]) + other).astype(jnp.bfloat16)
        return [rotated[key] for key in group]

    groups = [[(0, 0), (1, 0)], [(0, 2), (1, 2)], [(0, 1), (0, 3)], [(1, 1), (1, 3)]]
    fetched = [[[(0, 2)], [(1, 2)]], [[(0, 1), (0, 3)], [(1, 1)]], [[(1, 3)], []], [[], []]]
    sent = [[[], []], [[], []], [[], []], [[(0, 2)], [(0, 1), (0, 3)]]]

    due = []
    evens = []
    for at, group in enumerate(groups):
        gate = due
        stack = after(jnp.concatenate([pieces[key] for key in group], axis=0), gate)
        x, y = swap(stack, X), swap(stack, Y)
        due = [x, y] + [fetch(key, gate) for key in fetched[at][0]] + [send_back(key, gate) for key in sent[at][0]]
        if at:
            due += rotate(groups[at - 1], evens)
        gate = due
        to_x, to_y = after((y[tokens:], x[:tokens]), gate)
        xy = [swap(to_y, Y), swap(to_x, X)]
        due = xy + [fetch(key, gate) for key in fetched[at][1]] + [send_back(key, gate) for key in sent[at][1]]
        rows = [slice(0, tokens), slice(tokens, None)]
        evens = [jnp.concatenate([stack[r], x[r], y[r], last], axis=1) for r, last in zip(rows, xy)]

    send_back((1, 2), due)
    rotate(groups[-1], evens)
    for key in groups[-1]:
        send_back(key, [])

    total = []
    for side in (0, 1):
        kept = rotated[side, 0]
        for i in range(1, n_dp):
            kept = jnp.where(behind[side] == i, returned[side, i], kept)
        total.append(kept)
    all_rot_in = lax.all_gather(total[0], "tensor", axis=1, tiled=True)
    return product_and_divide(total[1], all_rot_in, eig_lambda, tokens)


def solution(mesh):
    placed = (
        P("dp", None, "tensor"),
        P("dp", None, "tensor"),
        P("dp", None, "tensor"),
        P("dp", None, "tensor"),
        P(),
        P("tensor", None),
    )
    n_dp, n_tensor = mesh.shape["dp"], mesh.shape["tensor"]

    def step(acts, *rest):
        whole = 2 * n_dp * acts.shape[1] * acts.shape[2] * n_tensor * acts.dtype.itemsize
        if whole <= ROOM and n_dp == 4 and n_tensor == X + Y + CORE + 1:
            return move_inputs(n_dp, acts, *rest)
        return move_bases(acts, *rest)

    return jax.shard_map(step, mesh=mesh, in_specs=placed, out_specs=P("dp", "tensor", None), check_vma=False)
```

```python
import jax
import jax.numpy as jnp
from jax import lax
from jax.sharding import PartitionSpec as P

damping = 0.01
ROOM = 2**25


def product_and_divide(rot_out, all_rot_in, eig_lambda, tokens):
    denom = eig_lambda.astype(jnp.float32) + damping
    contract = (((0,), (0,)), ((), ()))
    product = lax.dot_general(rot_out, all_rot_in, contract, preferred_element_type=jnp.float32) / tokens
    return (product / denom).astype(jnp.bfloat16)[None]


def from_owner(held, owner):
    return lax.psum(jnp.where(lax.axis_index("dp") == owner, held, jnp.zeros_like(held)), "dp")


def dot(a, b):
    return jnp.dot(a, b, preferred_element_type=jnp.float32)


def move_bases(acts, grads, basis_in_held, basis_out_held, owners, eig_lambda):
    column = lax.axis_index("tensor")
    basis_in = from_owner(basis_in_held[0], owners[0, column])
    basis_out = from_owner(basis_out_held[0], owners[1, column])
    rot_in = dot(lax.all_gather(acts[0], "tensor", axis=1, tiled=True), basis_in).astype(jnp.bfloat16)
    rot_out = dot(lax.all_gather(grads[0], "tensor", axis=1, tiled=True), basis_out).astype(jnp.bfloat16)
    return product_and_divide(
        rot_out, lax.all_gather(rot_in, "tensor", axis=1, tiled=True), eig_lambda, acts.shape[1]
    )


X, Y, CORE = 2, 4, 1


def swap(block, bit):
    return lax.ppermute(block, "tensor", [(j, j ^ bit) for j in range(X + Y + CORE + 1)])


def shift(block, by, n):
    return lax.ppermute(block, "dp", [(z, (z + by) % n) for z in range(n)])


def in_order(held, column, offsets):
    width = held.shape[0] // (X + Y + CORE + 1)
    blocks = [lax.dynamic_slice(held, ((column ^ i) * width, 0), (width, held.shape[1])) for i in offsets]
    return jnp.concatenate(blocks, axis=0)


def after(values, others):
    return lax.optimization_barrier((values, others))[0]


def move_inputs(n_dp, acts, grads, basis_in_held, basis_out_held, owners, eig_lambda):
    column = lax.axis_index("tensor")
    me = lax.axis_index("dp")
    own = (acts[0], grads[0])
    tokens = acts.shape[1]
    behind = [(me - owners[side, column]) % n_dp for side in (0, 1)]
    found = [0, X, Y, X + Y]
    held = (basis_in_held[0], basis_out_held[0])
    theirs = [swap(in_order(block, column, [CORE + i for i in found]), CORE) for block in held]
    ours = [in_order(block, column, found) for block in held]

    pieces = {(0, 0): own[0], (1, 0): own[1]}
    rotated = {}

    def fetch(side, i, gate):
        block, by = {1: (own[side], -1), 2: (pieces.get((side, 1)), -1), 3: (own[side], 1)}[i]
        pieces[side, i] = shift(after(block, gate), by, n_dp)
        return pieces[side, i]

    def rotate(group, evens):
        crossing = [swap(dot(even, theirs[side]), CORE) for (side, _), even in zip(group, evens)]
        for (side, i), even, other in zip(group, evens, crossing):
            rotated[side, i] = (dot(even, ours[side]) + other).astype(jnp.bfloat16)

    def pass_on(side):
        return shift(rotated[side, 2], 1, n_dp)

    def send_ahead(side, passed, gate):
        best = jnp.where(behind[side] == 0, rotated[side, 1], passed)
        return shift(after(best, gate), 1, n_dp)

    def send_behind(side):
        return shift(rotated[side, 3], -1, n_dp)

    def keep(side, from_behind, from_ahead):
        foreign = jnp.where(behind[side] == n_dp - 1, from_ahead, from_behind)
        return jnp.where(behind[side] == 0, rotated[side, 0], foreign)

    groups = [[(0, 0), (1, 0)], [(0, 1), (0, 2)], [(0, 3), (1, 2)], [(1, 1), (1, 3)]]
    due = []
    evens = []
    for at, group in enumerate(groups):
        gate = due
        stack = after(jnp.concatenate([pieces[key] for key in group], axis=0), gate)
        x, y = swap(stack, X), swap(stack, Y)
        due = [x, y]
        if at:
            rotate(groups[at - 1], evens)
        if at < 2:
            due += [fetch(at, 1, gate), fetch(at, 3, gate)]
        if at == 2:
            passed_in = pass_on(0)
            due += [passed_in, rotated[0, 1]]
        if at == 3:
            in_from_ahead = send_behind(0)
            passed_out = pass_on(1)
            due += [in_from_ahead, rotated[1, 2]]
        gate = due
        to_x, to_y = after((y[tokens:], x[:tokens]), gate)
        xy = [swap(to_y, Y), swap(to_x, X)]
        due = xy + []
        if at < 2:
            due.append(fetch(at, 2, gate))
        if at == 2:
            in_from_behind = send_ahead(0, passed_in, gate)
            due.append(in_from_behind)
        if at == 3:
            due.append(passed_out)
        rows = [slice(0, tokens), slice(tokens, None)]
        evens = [jnp.concatenate([stack[r], x[r], y[r], last], axis=1) for r, last in zip(rows, xy)]

    rot_in = keep(0, in_from_behind, in_from_ahead)
    all_rot_in = lax.all_gather(rot_in, "tensor", axis=1, tiled=True)
    rotate(groups[-1], evens)
    rot_out = keep(1, send_ahead(1, passed_out, []), send_behind(1))
    return product_and_divide(rot_out, all_rot_in, eig_lambda, tokens)


def solution(mesh):
    placed = (
        P("dp", None, "tensor"),
        P("dp", None, "tensor"),
        P("dp", None, "tensor"),
        P("dp", None, "tensor"),
        P(),
        P("tensor", None),
    )
    n_dp, n_tensor = mesh.shape["dp"], mesh.shape["tensor"]

    def step(acts, *rest):
        whole = 2 * n_dp * acts.shape[1] * acts.shape[2] * n_tensor * acts.dtype.itemsize
        if whole <= ROOM and n_dp == 4 and n_tensor == X + Y + CORE + 1:
            return move_inputs(n_dp, acts, *rest)
        return move_bases(acts, *rest)

    return jax.shard_map(step, mesh=mesh, in_specs=placed, out_specs=P("dp", "tensor", None), check_vma=False)
```

```python
import jax
import jax.numpy as jnp
from jax import lax
from jax.sharding import PartitionSpec as P

damping = 0.01
ROOM = 2**25


def product_and_divide(rot_out, all_rot_in, eig_lambda, tokens):
    denom = eig_lambda.astype(jnp.float32) + damping
    contract = (((0,), (0,)), ((), ()))
    product = lax.dot_general(rot_out, all_rot_in, contract, preferred_element_type=jnp.float32) / tokens
    return (product / denom).astype(jnp.bfloat16)[None]


def from_owner(held, owner):
    return lax.psum(jnp.where(lax.axis_index("dp") == owner, held, jnp.zeros_like(held)), "dp")


def dot(a, b):
    return jnp.dot(a, b, preferred_element_type=jnp.float32)


def move_bases(acts, grads, basis_in_held, basis_out_held, owners, eig_lambda):
    column = lax.axis_index("tensor")
    basis_in = from_owner(basis_in_held[0], owners[0, column])
    basis_out = from_owner(basis_out_held[0], owners[1, column])
    rot_in = dot(lax.all_gather(acts[0], "tensor", axis=1, tiled=True), basis_in).astype(jnp.bfloat16)
    rot_out = dot(lax.all_gather(grads[0], "tensor", axis=1, tiled=True), basis_out).astype(jnp.bfloat16)
    return product_and_divide(
        rot_out, lax.all_gather(rot_in, "tensor", axis=1, tiled=True), eig_lambda, acts.shape[1]
    )


X, Y, CORE = 2, 4, 1


def swap(block, bit):
    return lax.ppermute(block, "tensor", [(j, j ^ bit) for j in range(X + Y + CORE + 1)])


def shift(block, by, n):
    return lax.ppermute(block, "dp", [(z, (z + by) % n) for z in range(n)])


def in_order(held, column, offsets):
    width = held.shape[0] // (X + Y + CORE + 1)
    blocks = [lax.dynamic_slice(held, ((column ^ i) * width, 0), (width, held.shape[1])) for i in offsets]
    return jnp.concatenate(blocks, axis=0)


def after(values, others):
    return lax.optimization_barrier((values, others))[0]


def move_inputs(n_dp, acts, grads, basis_in_held, basis_out_held, owners, eig_lambda):
    column = lax.axis_index("tensor")
    me = lax.axis_index("dp")
    own = (acts[0], grads[0])
    tokens = acts.shape[1]
    behind = [(me - owners[side, column]) % n_dp for side in (0, 1)]
    found = [0, X, Y, X + Y]
    held = (basis_in_held[0], basis_out_held[0])
    theirs = [swap(in_order(block, column, [CORE + i for i in found]), CORE) for block in held]
    ours = [in_order(block, column, found) for block in held]

    pieces = {(0, 0): own[0], (1, 0): own[1]}
    rotated = {}

    def fetch(side, i, gate):
        block, by = {1: (own[side], -1), 2: (pieces.get((side, 1)), -1), 3: (own[side], 1)}[i]
        pieces[side, i] = shift(after(block, gate), by, n_dp)
        return pieces[side, i]

    def rotate(group, evens):
        crossing = [swap(dot(even, theirs[side]), CORE) for (side, _), even in zip(group, evens)]
        for (side, i), even, other in zip(group, evens, crossing):
            rotated[side, i] = (dot(even, ours[side]) + other).astype(jnp.bfloat16)
        return [rotated[key] for key in group]

    def pass_on(side):
        return shift(rotated[side, 2], 1, n_dp)

    def send_ahead(side, passed, gate):
        best = jnp.where(behind[side] == 0, rotated[side, 1], passed)
        return shift(after(best, gate), 1, n_dp)

    def send_behind(side):
        return shift(rotated[side, 3], -1, n_dp)

    def keep(side, from_behind, from_ahead):
        foreign = jnp.where(behind[side] == n_dp - 1, from_ahead, from_behind)
        return jnp.where(behind[side] == 0, rotated[side, 0], foreign)

    groups = [[(0, 0), (1, 0)], [(0, 1), (0, 2)], [(0, 3), (1, 2)], [(1, 1), (1, 3)]]
    due = []
    evens = []
    for at, group in enumerate(groups):
        gate = due
        stack = after(jnp.concatenate([pieces[key] for key in group], axis=0), gate)
        x, y = swap(stack, X), swap(stack, Y)
        due = [x, y]
        if at:
            due += rotate(groups[at - 1], evens)
        if at < 2:
            due += [fetch(at, 1, gate), fetch(at, 3, gate)]
        if at == 2:
            passed_in = pass_on(0)
            due.append(passed_in)
        if at == 3:
            in_from_ahead = send_behind(0)
            passed_out = pass_on(1)
            due.append(in_from_ahead)
        gate = due
        to_x, to_y = after((y[tokens:], x[:tokens]), gate)
        xy = [swap(to_y, Y), swap(to_x, X)]
        due = list(xy)
        if at < 2:
            due.append(fetch(at, 2, gate))
        if at == 2:
            in_from_behind = send_ahead(0, passed_in, gate)
            due.append(in_from_behind)
        if at == 3:
            due.append(passed_out)
        xy = after(xy, [])
        rows = [slice(0, tokens), slice(tokens, None)]
        evens = [jnp.concatenate([stack[r], x[r], y[r], last], axis=1) for r, last in zip(rows, xy)]

    rot_in = after(keep(0, in_from_behind, in_from_ahead), due)
    all_rot_in = lax.all_gather(rot_in, "tensor", axis=1, tiled=True)
    rotate(groups[-1], evens)
    rot_out = keep(1, send_ahead(1, passed_out, []), send_behind(1))
    return product_and_divide(rot_out, all_rot_in, eig_lambda, tokens)


def solution(mesh):
    placed = (
        P("dp", None, "tensor"),
        P("dp", None, "tensor"),
        P("dp", None, "tensor"),
        P("dp", None, "tensor"),
        P(),
        P("tensor", None),
    )
    n_dp, n_tensor = mesh.shape["dp"], mesh.shape["tensor"]

    def step(acts, *rest):
        whole = 2 * n_dp * acts.shape[1] * acts.shape[2] * n_tensor * acts.dtype.itemsize
        if whole <= ROOM and n_dp == 4 and n_tensor == X + Y + CORE + 1:
            return move_inputs(n_dp, acts, *rest)
        return move_bases(acts, *rest)

    return jax.shard_map(step, mesh=mesh, in_specs=placed, out_specs=P("dp", "tensor", None), check_vma=False)
```

```python
import jax
import jax.numpy as jnp
from jax import lax
from jax.sharding import PartitionSpec as P

damping = 0.01
ROOM = 2**25


def product_and_divide(rot_out, all_rot_in, eig_lambda, tokens):
    denom = eig_lambda.astype(jnp.float32) + damping
    contract = (((0,), (0,)), ((), ()))
    product = lax.dot_general(rot_out, all_rot_in, contract, preferred_element_type=jnp.float32) / tokens
    return (product / denom).astype(jnp.bfloat16)[None]


def from_owner(held, owner):
    return lax.psum(jnp.where(lax.axis_index("dp") == owner, held, jnp.zeros_like(held)), "dp")


def dot(a, b):
    return jnp.dot(a, b, preferred_element_type=jnp.float32)


def move_bases(acts, grads, basis_in_held, basis_out_held, owners, eig_lambda):
    column = lax.axis_index("tensor")
    basis_in = from_owner(basis_in_held[0], owners[0, column])
    basis_out = from_owner(basis_out_held[0], owners[1, column])
    rot_in = dot(lax.all_gather(acts[0], "tensor", axis=1, tiled=True), basis_in).astype(jnp.bfloat16)
    rot_out = dot(lax.all_gather(grads[0], "tensor", axis=1, tiled=True), basis_out).astype(jnp.bfloat16)
    return product_and_divide(
        rot_out, lax.all_gather(rot_in, "tensor", axis=1, tiled=True), eig_lambda, acts.shape[1]
    )


X, Y, CORE = 2, 4, 1


def swap(block, bit):
    return lax.ppermute(block, "tensor", [(j, j ^ bit) for j in range(X + Y + CORE + 1)])


def shift(block, by, n):
    return lax.ppermute(block, "dp", [(z, (z + by) % n) for z in range(n)])


def in_order(held, column, offsets):
    width = held.shape[0] // (X + Y + CORE + 1)
    blocks = [lax.dynamic_slice(held, ((column ^ i) * width, 0), (width, held.shape[1])) for i in offsets]
    return jnp.concatenate(blocks, axis=0)


def after(values, others):
    return lax.optimization_barrier((values, others))[0]


def move_inputs(n_dp, acts, grads, basis_in_held, basis_out_held, owners, eig_lambda):
    column = lax.axis_index("tensor")
    me = lax.axis_index("dp")
    own = (acts[0], grads[0])
    tokens = acts.shape[1]
    behind = [(me - owners[side, column]) % n_dp for side in (0, 1)]
    found = [0, X, Y, X + Y]
    held = (basis_in_held[0], basis_out_held[0])
    theirs = [swap(in_order(block, column, [CORE + i for i in found]), CORE) for block in held]
    ours = [in_order(block, column, found) for block in held]

    pieces = {(0, 0): own[0], (1, 0): own[1]}
    rotated = {}

    def fetch(side, i, gate):
        block, by = {1: (own[side], -1), 2: (pieces.get((side, 1)), -1), 3: (own[side], 1)}[i]
        pieces[side, i] = shift(after(block, gate), by, n_dp)
        return pieces[side, i]

    def rotate(group, evens):
        crossing = [swap(dot(even, theirs[side]), CORE) for (side, _), even in zip(group, evens)]
        for (side, i), even, other in zip(group, evens, crossing):
            rotated[side, i] = (dot(even, ours[side]) + other).astype(jnp.bfloat16)
        return [rotated[key] for key in group]

    def pass_on(side):
        return shift(rotated[side, 2], 1, n_dp)

    def send_ahead(side, passed, gate):
        best = jnp.where(behind[side] == 0, rotated[side, 1], passed)
        return shift(after(best, gate), 1, n_dp)

    def send_behind(side):
        return shift(rotated[side, 3], -1, n_dp)

    def keep(side, from_behind, from_ahead):
        foreign = jnp.where(behind[side] == n_dp - 1, from_ahead, from_behind)
        return jnp.where(behind[side] == 0, rotated[side, 0], foreign)

    groups = [[(0, 0), (1, 0)], [(0, 1), (0, 2)], [(0, 3), (1, 3)], [(1, 1), (1, 2)]]
    first, second = slice(0, tokens), slice(tokens, 2 * tokens)

    def slot(at, gate):
        to_x, to_y = [], []
        if at:
            stack, x, y = stacks[at - 1]
            to_x.append(y[second])
            to_y.append(x[first])
        if at < len(groups):
            new = jnp.concatenate([pieces[key] for key in groups[at]], axis=0)
            to_x.append(new)
            to_y.append(new)
        to_x, to_y = after((jnp.concatenate(to_x, axis=0), jnp.concatenate(to_y, axis=0)), gate)
        got = [swap(to_x, X), swap(to_y, Y)]
        from_x, from_y = after(got, [])
        if at:
            evens[at - 1] = [
                jnp.concatenate([stack[first], x[first], y[first], from_y[:tokens]], axis=1),
                jnp.concatenate([stack[second], x[second], y[second], from_x[:tokens]], axis=1),
            ]
        if at < len(groups):
            stacks[at] = (new, from_x[-2 * tokens :], from_y[-2 * tokens :])
        return got

    stacks, evens = {}, {}
    due = slot(0, [])
    due += [fetch(0, 1, []), fetch(0, 2, [])]

    gate, due = due, slot(1, due)
    due += [fetch(0, 3, gate), fetch(1, 3, gate), fetch(1, 1, gate)]

    gate, due = due, slot(2, due)
    due += [fetch(1, 2, gate)] + rotate(groups[0], evens[0])

    gate, due = due, slot(3, due)
    due += rotate(groups[1], evens[1])
    passed_in = pass_on(0)
    due.append(passed_in)

    gate, due = due, slot(4, due)
    due += rotate(groups[2], evens[2])
    in_from_behind = send_ahead(0, passed_in, gate)
    rot_in = after(keep(0, in_from_behind, send_behind(0)), due)
    all_rot_in = lax.all_gather(rot_in, "tensor", axis=1, tiled=True)

    out_from_ahead = send_behind(1)
    rotate(groups[3], evens[3])
    rot_out = keep(1, send_ahead(1, pass_on(1), []), out_from_ahead)
    return product_and_divide(rot_out, all_rot_in, eig_lambda, tokens)


def solution(mesh):
    placed = (
        P("dp", None, "tensor"),
        P("dp", None, "tensor"),
        P("dp", None, "tensor"),
        P("dp", None, "tensor"),
        P(),
        P("tensor", None),
    )
    n_dp, n_tensor = mesh.shape["dp"], mesh.shape["tensor"]

    def step(acts, *rest):
        whole = 2 * n_dp * acts.shape[1] * acts.shape[2] * n_tensor * acts.dtype.itemsize
        if whole <= ROOM and n_dp == 4 and n_tensor == X + Y + CORE + 1:
            return move_inputs(n_dp, acts, *rest)
        return move_bases(acts, *rest)

    return jax.shard_map(step, mesh=mesh, in_specs=placed, out_specs=P("dp", "tensor", None), check_vma=False)
```

```python
import jax
import jax.numpy as jnp
from jax import lax
from jax.sharding import PartitionSpec as P

damping = 0.01
ROOM = 2**25


def product_and_divide(rot_out, all_rot_in, eig_lambda, tokens):
    denom = eig_lambda.astype(jnp.float32) + damping
    contract = (((0,), (0,)), ((), ()))
    product = lax.dot_general(rot_out, all_rot_in, contract, preferred_element_type=jnp.float32) / tokens
    return (product / denom).astype(jnp.bfloat16)[None]


def from_owner(held, owner):
    return lax.psum(jnp.where(lax.axis_index("dp") == owner, held, jnp.zeros_like(held)), "dp")


def dot(a, b):
    return jnp.dot(a, b, preferred_element_type=jnp.float32)


def move_bases(acts, grads, basis_in_held, basis_out_held, owners, eig_lambda):
    column = lax.axis_index("tensor")
    basis_in = from_owner(basis_in_held[0], owners[0, column])
    basis_out = from_owner(basis_out_held[0], owners[1, column])
    rot_in = dot(lax.all_gather(acts[0], "tensor", axis=1, tiled=True), basis_in).astype(jnp.bfloat16)
    rot_out = dot(lax.all_gather(grads[0], "tensor", axis=1, tiled=True), basis_out).astype(jnp.bfloat16)
    return product_and_divide(
        rot_out, lax.all_gather(rot_in, "tensor", axis=1, tiled=True), eig_lambda, acts.shape[1]
    )


X, Y, CORE = 2, 4, 1


def swap(block, bit):
    return lax.ppermute(block, "tensor", [(j, j ^ bit) for j in range(X + Y + CORE + 1)])


def shift(block, by, n):
    return lax.ppermute(block, "dp", [(z, (z + by) % n) for z in range(n)])


def in_order(held, column, offsets):
    width = held.shape[0] // (X + Y + CORE + 1)
    blocks = [lax.dynamic_slice(held, ((column ^ i) * width, 0), (width, held.shape[1])) for i in offsets]
    return jnp.concatenate(blocks, axis=0)


def after(values, others):
    return lax.optimization_barrier((values, others))[0]


def move_inputs(n_dp, acts, grads, basis_in_held, basis_out_held, owners, eig_lambda):
    column = lax.axis_index("tensor")
    me = lax.axis_index("dp")
    own = (acts[0], grads[0])
    tokens = acts.shape[1]
    behind = [(me - owners[side, column]) % n_dp for side in (0, 1)]
    found = [0, X, Y, X + Y]
    held = (basis_in_held[0], basis_out_held[0])
    ours = [in_order(block, column, found) for block in held]
    theirs = jnp.split(swap(jnp.concatenate([in_order(block, column, [CORE + i for i in found]) for block in held]), CORE), 2)

    pieces = {(0, 0): own[0], (1, 0): own[1]}
    rotated = {}

    def fetch(side, i, gate):
        block, by = {1: (own[side], -1), 2: (pieces.get((side, 1)), -1), 3: (own[side], 1)}[i]
        pieces[side, i] = shift(after(block, gate), by, n_dp)
        return pieces[side, i]

    def rotate(group, evens):
        crossing = [swap(dot(even, theirs[side]), CORE) for (side, _), even in zip(group, evens)]
        for (side, i), even, other in zip(group, evens, crossing):
            rotated[side, i] = (dot(even, ours[side]) + other).astype(jnp.bfloat16)
        return [rotated[key] for key in group]

    def pass_on(side):
        return shift(rotated[side, 2], 1, n_dp)

    def send_ahead(side, passed, gate):
        best = jnp.where(behind[side] == 0, rotated[side, 1], passed)
        return shift(after(best, gate), 1, n_dp)

    def send_behind(side):
        return shift(rotated[side, 3], -1, n_dp)

    def keep(side, from_behind, from_ahead):
        foreign = jnp.where(behind[side] == n_dp - 1, from_ahead, from_behind)
        return jnp.where(behind[side] == 0, rotated[side, 0], foreign)

    groups = [[(0, 0), (1, 0)], [(0, 1), (0, 2)], [(0, 3), (1, 2)], [(1, 1), (1, 3)]]
    first, second = slice(0, tokens), slice(tokens, 2 * tokens)

    def slot(at, gate):
        to_x, to_y = [], []
        if at:
            stack, x, y = stacks[at - 1]
            to_x.append(y[second])
            to_y.append(x[first])
        if at < len(groups):
            new = jnp.concatenate([pieces[key] for key in groups[at]], axis=0)
            to_x.append(new)
            to_y.append(new)
        to_x, to_y = after((jnp.concatenate(to_x, axis=0), jnp.concatenate(to_y, axis=0)), gate)
        got = [swap(to_x, X), swap(to_y, Y)]
        from_x, from_y = after(got, [])
        if at:
            evens[at - 1] = [
                jnp.concatenate([stack[first], x[first], y[first], from_y[:tokens]], axis=1),
                jnp.concatenate([stack[second], x[second], y[second], from_x[:tokens]], axis=1),
            ]
        if at < len(groups):
            stacks[at] = (new, from_x[-2 * tokens :], from_y[-2 * tokens :])
        return got

    stacks, evens = {}, {}
    due = slot(0, [])
    due += [fetch(0, 1, []), fetch(0, 2, [])]

    gate, due = due, slot(1, due)
    due += [fetch(0, 3, gate), fetch(1, 1, gate), fetch(1, 2, gate)]

    def begun(at, gate):
        corner = after(stacks[at][1][:16, :128], gate)
        return after(evens[at], swap(corner, CORE))

    gate, due = due, slot(2, due)
    due += [fetch(1, 3, gate)] + rotate(groups[0], begun(0, gate))

    gate, due = due, slot(3, due)
    due += rotate(groups[1], begun(1, gate))
    in_from_behind = send_ahead(0, pass_on(0), [])
    due.append(in_from_behind)

    gate, due = due, slot(4, due)
    rotate(groups[2], begun(2, gate))
    rot_in = after(keep(0, in_from_behind, send_behind(0)), due)
    all_rot_in = lax.all_gather(rot_in, "tensor", axis=1, tiled=True)

    passed_out = pass_on(1)
    rotate(groups[3], evens[3])
    rot_out = keep(1, send_ahead(1, passed_out, []), send_behind(1))
    return product_and_divide(rot_out, all_rot_in, eig_lambda, tokens)


def solution(mesh):
    placed = (
        P("dp", None, "tensor"),
        P("dp", None, "tensor"),
        P("dp", None, "tensor"),
        P("dp", None, "tensor"),
        P(),
        P("tensor", None),
    )
    n_dp, n_tensor = mesh.shape["dp"], mesh.shape["tensor"]

    def step(acts, *rest):
        whole = 2 * n_dp * acts.shape[1] * acts.shape[2] * n_tensor * acts.dtype.itemsize
        if whole <= ROOM and n_dp == 4 and n_tensor == X + Y + CORE + 1:
            return move_inputs(n_dp, acts, *rest)
        return move_bases(acts, *rest)

    return jax.shard_map(step, mesh=mesh, in_specs=placed, out_specs=P("dp", "tensor", None), check_vma=False)
```

```python
import jax
import jax.numpy as jnp
from jax import lax
from jax.sharding import PartitionSpec as P

damping = 0.01
ROOM = 2**25


def product_and_divide(rot_out, all_rot_in, eig_lambda, tokens):
    denom = eig_lambda.astype(jnp.float32) + damping
    contract = (((0,), (0,)), ((), ()))
    product = lax.dot_general(rot_out, all_rot_in, contract, preferred_element_type=jnp.float32) / tokens
    return (product / denom).astype(jnp.bfloat16)[None]


def from_owner(held, owner):
    return lax.psum(jnp.where(lax.axis_index("dp") == owner, held, jnp.zeros_like(held)), "dp")


def dot(a, b):
    return jnp.dot(a, b, preferred_element_type=jnp.float32)


def move_bases(acts, grads, basis_in_held, basis_out_held, owners, eig_lambda):
    column = lax.axis_index("tensor")
    basis_in = from_owner(basis_in_held[0], owners[0, column])
    basis_out = from_owner(basis_out_held[0], owners[1, column])
    rot_in = dot(lax.all_gather(acts[0], "tensor", axis=1, tiled=True), basis_in).astype(jnp.bfloat16)
    rot_out = dot(lax.all_gather(grads[0], "tensor", axis=1, tiled=True), basis_out).astype(jnp.bfloat16)
    return product_and_divide(
        rot_out, lax.all_gather(rot_in, "tensor", axis=1, tiled=True), eig_lambda, acts.shape[1]
    )


X, Y, CORE = 2, 4, 1


def swap(block, bit):
    return lax.ppermute(block, "tensor", [(j, j ^ bit) for j in range(X + Y + CORE + 1)])


def shift(block, by, n):
    return lax.ppermute(block, "dp", [(z, (z + by) % n) for z in range(n)])


def in_order(held, column, offsets):
    width = held.shape[0] // (X + Y + CORE + 1)
    blocks = [lax.dynamic_slice(held, ((column ^ i) * width, 0), (width, held.shape[1])) for i in offsets]
    return jnp.concatenate(blocks, axis=0)


def after(values, others):
    return lax.optimization_barrier((values, others))[0]


def move_inputs(n_dp, acts, grads, basis_in_held, basis_out_held, owners, eig_lambda):
    column = lax.axis_index("tensor")
    me = lax.axis_index("dp")
    own = (acts[0], grads[0])
    tokens = acts.shape[1]
    behind = [(me - owners[side, column]) % n_dp for side in (0, 1)]
    found = [0, X, Y, X + Y]
    held = (basis_in_held[0], basis_out_held[0])
    ours = [in_order(block, column, found) for block in held]
    theirs = jnp.split(swap(jnp.concatenate([in_order(block, column, [CORE + i for i in found]) for block in held]), CORE), 2)

    pieces = {(0, 0): own[0], (1, 0): own[1]}
    rotated = {}

    def fetch(side, i, gate):
        block, by = {1: (own[side], -1), 2: (pieces.get((side, 1)), -1), 3: (own[side], 1)}[i]
        pieces[side, i] = shift(after(block, gate), by, n_dp)
        return pieces[side, i]

    def rotate(group, evens):
        crossing = [swap(dot(even, theirs[side]), CORE) for (side, _), even in zip(group, evens)]
        for (side, i), even, other in zip(group, evens, crossing):
            rotated[side, i] = (dot(even, ours[side]) + other).astype(jnp.bfloat16)
        return [rotated[key] for key in group]

    def pass_on(side):
        return shift(rotated[side, 2], 1, n_dp)

    def send_ahead(side, passed, gate):
        best = jnp.where(behind[side] == 0, rotated[side, 1], passed)
        return shift(after(best, gate), 1, n_dp)

    def send_behind(side):
        return shift(rotated[side, 3], -1, n_dp)

    def keep(side, from_behind, from_ahead):
        foreign = jnp.where(behind[side] == n_dp - 1, from_ahead, from_behind)
        return jnp.where(behind[side] == 0, rotated[side, 0], foreign)

    groups = [[(0, 0), (1, 0)], [(0, 1), (0, 2)], [(0, 3), (1, 2)], [(1, 1), (1, 3)]]
    first, second = slice(0, tokens), slice(tokens, 2 * tokens)

    def slot(at, gate):
        to_x, to_y = [], []
        if at:
            stack, x, y = stacks[at - 1]
            to_x.append(y[second])
            to_y.append(x[first])
        if at < len(groups):
            new = jnp.concatenate([pieces[key] for key in groups[at]], axis=0)
            to_x.append(new)
            to_y.append(new)
        to_x, to_y = after((jnp.concatenate(to_x, axis=0), jnp.concatenate(to_y, axis=0)), gate)
        got = [swap(to_x, X), swap(to_y, Y)]
        from_x, from_y = after(got, [])
        if at:
            evens[at - 1] = [
                jnp.concatenate([stack[first], x[first], y[first], from_y[:tokens]], axis=1),
                jnp.concatenate([stack[second], x[second], y[second], from_x[:tokens]], axis=1),
            ]
        if at < len(groups):
            stacks[at] = (new, from_x[-2 * tokens :], from_y[-2 * tokens :])
        return got

    stacks, evens = {}, {}
    due = slot(0, [])
    due += [fetch(0, 1, []), fetch(0, 2, [])]

    gate, due = due, slot(1, due)
    due += [fetch(0, 3, gate), fetch(1, 1, gate), fetch(1, 2, gate)]

    def begun(at, gate):
        corner = after(stacks[at][1][:16, :128], gate)
        return after(evens[at], swap(corner, CORE))

    gate, due = due, slot(2, due)
    due += [fetch(1, 3, gate)] + rotate(groups[0], begun(0, gate))

    gate, due = due, slot(3, due)
    rotate(groups[1], begun(1, gate))
    passed_in = pass_on(0)
    due.append(passed_in)

    gate, due = due, slot(4, due)
    in_from_behind = send_ahead(0, passed_in, gate)
    ready = rotate(groups[2], begun(2, gate))
    in_from_ahead = send_behind(0)
    passed_out = pass_on(1)
    ready += rotate(groups[3], after(evens[3], due))
    rot_in = after(keep(0, in_from_behind, in_from_ahead), ready)
    all_rot_in = lax.all_gather(rot_in, "tensor", axis=1, tiled=True)
    rot_out = keep(1, send_ahead(1, passed_out, []), send_behind(1))
    return product_and_divide(rot_out, all_rot_in, eig_lambda, tokens)


def solution(mesh):
    placed = (
        P("dp", None, "tensor"),
        P("dp", None, "tensor"),
        P("dp", None, "tensor"),
        P("dp", None, "tensor"),
        P(),
        P("tensor", None),
    )
    n_dp, n_tensor = mesh.shape["dp"], mesh.shape["tensor"]

    def step(acts, *rest):
        whole = 2 * n_dp * acts.shape[1] * acts.shape[2] * n_tensor * acts.dtype.itemsize
        if whole <= ROOM and n_dp == 4 and n_tensor == X + Y + CORE + 1:
            return move_inputs(n_dp, acts, *rest)
        return move_bases(acts, *rest)

    return jax.shard_map(step, mesh=mesh, in_specs=placed, out_specs=P("dp", "tensor", None), check_vma=False)
```

```python
import jax
import jax.numpy as jnp
from jax import lax
from jax.sharding import PartitionSpec as P

damping = 0.01
ROOM = 2**25


def product_and_divide(rot_out, all_rot_in, eig_lambda, tokens):
    denom = eig_lambda.astype(jnp.float32) + damping
    contract = (((0,), (0,)), ((), ()))
    product = lax.dot_general(rot_out, all_rot_in, contract, preferred_element_type=jnp.float32) / tokens
    return (product / denom).astype(jnp.bfloat16)[None]


def from_owner(held, owner):
    return lax.psum(jnp.where(lax.axis_index("dp") == owner, held, jnp.zeros_like(held)), "dp")


def dot(a, b):
    return jnp.dot(a, b, preferred_element_type=jnp.float32)


def move_bases(acts, grads, basis_in_held, basis_out_held, owners, eig_lambda):
    column = lax.axis_index("tensor")
    basis_in = from_owner(basis_in_held[0], owners[0, column])
    basis_out = from_owner(basis_out_held[0], owners[1, column])
    rot_in = dot(lax.all_gather(acts[0], "tensor", axis=1, tiled=True), basis_in).astype(jnp.bfloat16)
    rot_out = dot(lax.all_gather(grads[0], "tensor", axis=1, tiled=True), basis_out).astype(jnp.bfloat16)
    return product_and_divide(
        rot_out, lax.all_gather(rot_in, "tensor", axis=1, tiled=True), eig_lambda, acts.shape[1]
    )


X, Y, CORE = 2, 4, 1


def swap(block, bit):
    return lax.ppermute(block, "tensor", [(j, j ^ bit) for j in range(X + Y + CORE + 1)])


def shift(block, by, n):
    return lax.ppermute(block, "dp", [(z, (z + by) % n) for z in range(n)])


def in_order(held, column, offsets):
    width = held.shape[0] // (X + Y + CORE + 1)
    blocks = [lax.dynamic_slice(held, ((column ^ i) * width, 0), (width, held.shape[1])) for i in offsets]
    return jnp.concatenate(blocks, axis=0)


def after(values, others):
    return lax.optimization_barrier((values, others))[0]


def move_inputs(n_dp, acts, grads, basis_in_held, basis_out_held, owners, eig_lambda):
    column = lax.axis_index("tensor")
    me = lax.axis_index("dp")
    own = (acts[0], grads[0])
    tokens = acts.shape[1]
    behind = [(me - owners[side, column]) % n_dp for side in (0, 1)]
    found = [0, X, Y, X + Y]
    held = (basis_in_held[0], basis_out_held[0])
    ours = [in_order(block, column, found) for block in held]
    theirs = [swap(in_order(block, column, [CORE + i for i in found]), CORE) for block in held]

    pieces = {(0, 0): own[0], (1, 0): own[1]}
    rotated = {}

    def fetch(side, i, gate):
        block, by = {1: (own[side], -1), 2: (pieces.get((side, 1)), -1), 3: (own[side], 1)}[i]
        pieces[side, i] = shift(after(block, gate), by, n_dp)
        return pieces[side, i]

    def rotate(group, evens):
        crossing = [swap(dot(even, theirs[side]), CORE) for (side, _), even in zip(group, evens)]
        for (side, i), even, other in zip(group, evens, crossing):
            rotated[side, i] = (dot(even, ours[side]) + other).astype(jnp.bfloat16)
        return [rotated[key] for key in group]

    def pass_on(side):
        return shift(rotated[side, 2], 1, n_dp)

    def send_ahead(side, passed, gate):
        best = jnp.where(behind[side] == 0, rotated[side, 1], passed)
        return shift(after(best, gate), 1, n_dp)

    def send_behind(side):
        return shift(rotated[side, 3], -1, n_dp)

    def keep(side, from_behind, from_ahead):
        foreign = jnp.where(behind[side] == n_dp - 1, from_ahead, from_behind)
        return jnp.where(behind[side] == 0, rotated[side, 0], foreign)

    groups = [[(0, 0), (1, 0)], [(0, 1), (0, 2)], [(0, 3), (1, 2)], [(1, 1), (1, 3)]]
    first, second = slice(0, tokens), slice(tokens, 2 * tokens)

    def slot(at, gate):
        to_x, to_y = [], []
        if at:
            stack, x, y = stacks[at - 1]
            to_x.append(y[second])
            to_y.append(x[first])
        if at < len(groups):
            new = jnp.concatenate([pieces[key] for key in groups[at]], axis=0)
            to_x.append(new)
            to_y.append(new)
        to_x, to_y = after((jnp.concatenate(to_x, axis=0), jnp.concatenate(to_y, axis=0)), gate)
        got = [swap(to_x, X), swap(to_y, Y)]
        from_x, from_y = after(got, [])
        if at:
            evens[at - 1] = [
                jnp.concatenate([stack[first], x[first], y[first], from_y[:tokens]], axis=1),
                jnp.concatenate([stack[second], x[second], y[second], from_x[:tokens]], axis=1),
            ]
        if at < len(groups):
            stacks[at] = (new, from_x[-2 * tokens :], from_y[-2 * tokens :])
        return got

    stacks, evens = {}, {}
    due = slot(0, [])
    due += [fetch(0, 1, []), fetch(0, 2, [])] + theirs

    gate, due = due, slot(1, due)
    due += [fetch(0, 3, gate), fetch(1, 1, gate), fetch(1, 2, gate)]

    def begun(at, gate):
        corner = after(stacks[at][1][:16, :128], gate)
        return after(evens[at], swap(corner, CORE))

    gate, due = due, slot(2, due)
    due += [fetch(1, 3, gate)] + rotate(groups[0], begun(0, gate))

    gate, due = due, slot(3, due)
    rotate(groups[1], begun(1, gate))
    passed_in = pass_on(0)
    due.append(passed_in)

    gate, due = due, slot(4, due)
    in_from_behind = send_ahead(0, passed_in, gate)
    ready = rotate(groups[2], begun(2, gate))
    in_from_ahead = send_behind(0)
    passed_out = pass_on(1)
    ready += rotate(groups[3], after(evens[3], due))
    rot_in = after(keep(0, in_from_behind, in_from_ahead), ready)
    all_rot_in = lax.all_gather(rot_in, "tensor", axis=1, tiled=True)
    rot_out = keep(1, send_ahead(1, passed_out, []), send_behind(1))
    return product_and_divide(rot_out, all_rot_in, eig_lambda, tokens)


def solution(mesh):
    placed = (
        P("dp", None, "tensor"),
        P("dp", None, "tensor"),
        P("dp", None, "tensor"),
        P("dp", None, "tensor"),
        P(),
        P("tensor", None),
    )
    n_dp, n_tensor = mesh.shape["dp"], mesh.shape["tensor"]

    def step(acts, *rest):
        whole = 2 * n_dp * acts.shape[1] * acts.shape[2] * n_tensor * acts.dtype.itemsize
        if whole <= ROOM and n_dp == 4 and n_tensor == X + Y + CORE + 1:
            return move_inputs(n_dp, acts, *rest)
        return move_bases(acts, *rest)

    return jax.shard_map(step, mesh=mesh, in_specs=placed, out_specs=P("dp", "tensor", None), check_vma=False)
```

```python
import jax
import jax.numpy as jnp
from jax import lax
from jax.sharding import PartitionSpec as P

damping = 0.01
ROOM = 2**25


def product_and_divide(rot_out, all_rot_in, eig_lambda, tokens):
    denom = eig_lambda.astype(jnp.float32) + damping
    contract = (((0,), (0,)), ((), ()))
    product = lax.dot_general(rot_out, all_rot_in, contract, preferred_element_type=jnp.float32) / tokens
    return (product / denom).astype(jnp.bfloat16)[None]


def from_owner(held, owner):
    return lax.psum(jnp.where(lax.axis_index("dp") == owner, held, jnp.zeros_like(held)), "dp")


def dot(a, b):
    return jnp.dot(a, b, preferred_element_type=jnp.float32)


def move_bases(acts, grads, basis_in_held, basis_out_held, owners, eig_lambda):
    column = lax.axis_index("tensor")
    basis_in = from_owner(basis_in_held[0], owners[0, column])
    basis_out = from_owner(basis_out_held[0], owners[1, column])
    rot_in = dot(lax.all_gather(acts[0], "tensor", axis=1, tiled=True), basis_in).astype(jnp.bfloat16)
    rot_out = dot(lax.all_gather(grads[0], "tensor", axis=1, tiled=True), basis_out).astype(jnp.bfloat16)
    return product_and_divide(
        rot_out, lax.all_gather(rot_in, "tensor", axis=1, tiled=True), eig_lambda, acts.shape[1]
    )


X, Y, CORE = 2, 4, 1


def swap(block, bit):
    return lax.ppermute(block, "tensor", [(j, j ^ bit) for j in range(X + Y + CORE + 1)])


def shift(block, by, n):
    return lax.ppermute(block, "dp", [(z, (z + by) % n) for z in range(n)])


def in_order(held, column, offsets):
    width = held.shape[0] // (X + Y + CORE + 1)
    blocks = [lax.dynamic_slice(held, ((column ^ i) * width, 0), (width, held.shape[1])) for i in offsets]
    return jnp.concatenate(blocks, axis=0)


def after(values, others):
    return lax.optimization_barrier((values, others))[0]


def move_inputs(n_dp, acts, grads, basis_in_held, basis_out_held, owners, eig_lambda):
    column = lax.axis_index("tensor")
    me = lax.axis_index("dp")
    own = (acts[0], grads[0])
    tokens = acts.shape[1]
    behind = [(me - owners[side, column]) % n_dp for side in (0, 1)]
    pieces = {(0, 0): own[0], (1, 0): own[1]}
    rotated = {}

    def fetch(side, i, gate):
        block, by = {1: (own[side], -1), 2: (pieces.get((side, 1)), -1), 3: (own[side], 1)}[i]
        pieces[side, i] = shift(after(block, gate), by, n_dp)
        return pieces[side, i]

    def cross(group, evens, gate):
        halves = [dot(even, theirs[side]) for (side, _), even in zip(group, evens)]
        return [swap(block, CORE) for block in after(halves, gate)]

    def rotate(group, evens, crossed=None):
        crossed = cross(group, evens, []) if crossed is None else crossed
        for (side, i), even, other in zip(group, evens, crossed):
            rotated[side, i] = (dot(even, ours[side]) + other).astype(jnp.bfloat16)
        return [rotated[key] for key in group]

    def pass_on(side):
        return shift(rotated[side, 2], 1, n_dp)

    def send_ahead(side, passed, gate):
        best = jnp.where(behind[side] == 0, rotated[side, 1], passed)
        return shift(after(best, gate), 1, n_dp)

    def send_behind(side):
        return shift(rotated[side, 3], -1, n_dp)

    def keep(side, from_behind, from_ahead):
        foreign = jnp.where(behind[side] == n_dp - 1, from_ahead, from_behind)
        return jnp.where(behind[side] == 0, rotated[side, 0], foreign)

    groups = [[(0, 0), (1, 0)], [(0, 1), (0, 2)], [(0, 3), (1, 2)], [(1, 1), (1, 3)]]
    first, second = slice(0, tokens), slice(tokens, 2 * tokens)

    def slot(at, gate):
        to_x, to_y = [], []
        if at:
            stack, x, y = stacks[at - 1]
            to_x.append(y[second])
            to_y.append(x[first])
        if at < len(groups):
            new = jnp.concatenate([pieces[key] for key in groups[at]], axis=0)
            to_x.append(new)
            to_y.append(new)
        to_x, to_y = after((jnp.concatenate(to_x, axis=0), jnp.concatenate(to_y, axis=0)), gate)
        got = [swap(to_x, X), swap(to_y, Y)]
        from_x, from_y = after(got, [])
        if at:
            evens[at - 1] = [
                jnp.concatenate([stack[first], x[first], y[first], from_y[:tokens]], axis=1),
                jnp.concatenate([stack[second], x[second], y[second], from_x[:tokens]], axis=1),
            ]
        if at < len(groups):
            stacks[at] = (new, from_x[-2 * tokens :], from_y[-2 * tokens :])
        return got

    stacks, evens = {}, {}
    due = slot(0, [])
    due += [fetch(0, 1, []), fetch(0, 2, [])]
    found = [0, X, Y, X + Y]
    held = after([basis_in_held[0], basis_out_held[0]], pieces[0, 1])
    theirs = [swap(in_order(block, column, [CORE + i for i in found]), CORE) for block in held]
    ours = [in_order(block, column, found) for block in held]
    due += theirs

    gate, due = due, slot(1, due)
    due += [fetch(0, 3, gate), fetch(1, 1, gate), fetch(1, 2, gate)]

    gate, due = due, slot(2, due)
    due += [fetch(1, 3, gate)]
    evens[0] = after(evens[0], pieces[1, 3])

    crossed = cross(groups[0], evens[0], due)
    gate, due = due, slot(3, due)
    rotate(groups[1], after(evens[1], crossed))
    rotate(groups[0], evens[0], crossed)
    passed_in = pass_on(0)
    due.append(passed_in)

    gate, due = due, slot(4, due)
    in_from_behind = send_ahead(0, passed_in, gate)
    rotate(groups[2], evens[2])
    in_from_ahead = send_behind(0)
    passed_out = pass_on(1)
    rotate(groups[3], after(evens[3], [rotated[key] for key in groups[2]]))
    rot_in = after(keep(0, in_from_behind, in_from_ahead), due)
    all_rot_in = lax.all_gather(rot_in, "tensor", axis=1, tiled=True)
    rot_out = keep(1, send_ahead(1, passed_out, []), send_behind(1))
    return product_and_divide(rot_out, all_rot_in, eig_lambda, tokens)


def solution(mesh):
    placed = (
        P("dp", None, "tensor"),
        P("dp", None, "tensor"),
        P("dp", None, "tensor"),
        P("dp", None, "tensor"),
        P(),
        P("tensor", None),
    )
    n_dp, n_tensor = mesh.shape["dp"], mesh.shape["tensor"]

    def step(acts, *rest):
        whole = 2 * n_dp * acts.shape[1] * acts.shape[2] * n_tensor * acts.dtype.itemsize
        if whole <= ROOM and n_dp == 4 and n_tensor == X + Y + CORE + 1:
            return move_inputs(n_dp, acts, *rest)
        return move_bases(acts, *rest)

    return jax.shard_map(step, mesh=mesh, in_specs=placed, out_specs=P("dp", "tensor", None), check_vma=False)
```

```python
import jax
import jax.numpy as jnp
from jax import lax
from jax.sharding import PartitionSpec as P

damping = 0.01
ROOM = 2**25


def product_and_divide(rot_out, all_rot_in, eig_lambda, tokens):
    denom = eig_lambda.astype(jnp.float32) + damping
    contract = (((0,), (0,)), ((), ()))
    product = lax.dot_general(rot_out, all_rot_in, contract, preferred_element_type=jnp.float32) / tokens
    return (product / denom).astype(jnp.bfloat16)[None]


def from_owner(held, owner):
    return lax.psum(jnp.where(lax.axis_index("dp") == owner, held, jnp.zeros_like(held)), "dp")


def dot(a, b):
    return jnp.dot(a, b, preferred_element_type=jnp.float32)


def move_bases(acts, grads, basis_in_held, basis_out_held, owners, eig_lambda):
    column = lax.axis_index("tensor")
    basis_in = from_owner(basis_in_held[0], owners[0, column])
    basis_out = from_owner(basis_out_held[0], owners[1, column])
    rot_in = dot(lax.all_gather(acts[0], "tensor", axis=1, tiled=True), basis_in).astype(jnp.bfloat16)
    rot_out = dot(lax.all_gather(grads[0], "tensor", axis=1, tiled=True), basis_out).astype(jnp.bfloat16)
    return product_and_divide(
        rot_out, lax.all_gather(rot_in, "tensor", axis=1, tiled=True), eig_lambda, acts.shape[1]
    )


X, Y, CORE = 2, 4, 1


def swap(block, bit):
    return lax.ppermute(block, "tensor", [(j, j ^ bit) for j in range(X + Y + CORE + 1)])


def shift(block, by, n):
    return lax.ppermute(block, "dp", [(z, (z + by) % n) for z in range(n)])


def in_order(held, column, offsets):
    width = held.shape[0] // (X + Y + CORE + 1)
    blocks = [lax.dynamic_slice(held, ((column ^ i) * width, 0), (width, held.shape[1])) for i in offsets]
    return jnp.concatenate(blocks, axis=0)


def after(values, others):
    return lax.optimization_barrier((values, others))[0]


def move_inputs(n_dp, acts, grads, basis_in_held, basis_out_held, owners, eig_lambda):
    column = lax.axis_index("tensor")
    me = lax.axis_index("dp")
    own = (acts[0], grads[0])
    tokens = acts.shape[1]
    behind = [(me - owners[side, column]) % n_dp for side in (0, 1)]
    pieces = {(0, 0): own[0], (1, 0): own[1]}
    rotated = {}

    def fetch(side, i, gate):
        block, by = {1: (own[side], -1), 2: (pieces.get((side, 1)), -1), 3: (own[side], 1)}[i]
        pieces[side, i] = shift(after(block, gate), by, n_dp)
        return pieces[side, i]

    def half_product(key, even):
        return dot(even, theirs[key[0]])

    def rotate(key, even, crossed):
        rotated[key] = (dot(even, ours[key[0]]) + crossed).astype(jnp.bfloat16)

    def cross(block, gate):
        return swap(after(block, gate), CORE)

    def pass_on(side):
        return shift(rotated[side, 2], 1, n_dp)

    def send_ahead(side, passed, gate):
        best = jnp.where(behind[side] == 0, rotated[side, 1], passed)
        return shift(after(best, gate), 1, n_dp)

    def send_behind(side):
        return shift(rotated[side, 3], -1, n_dp)

    def keep(side, from_behind, from_ahead):
        foreign = jnp.where(behind[side] == n_dp - 1, from_ahead, from_behind)
        return jnp.where(behind[side] == 0, rotated[side, 0], foreign)

    groups = [[(0, 0), (1, 0)], [(0, 1), (0, 2)], [(0, 3), (1, 2)], [(1, 1), (1, 3)]]
    first, second = slice(0, tokens), slice(tokens, 2 * tokens)

    def begin(at, gate):
        to_x, to_y = [], []
        if at:
            _, x, y = stacks[at - 1]
            to_x.append(y[second])
            to_y.append(x[first])
        if at < len(groups):
            stacks[at] = jnp.concatenate([pieces[key] for key in groups[at]], axis=0)
            to_x.append(stacks[at])
            to_y.append(stacks[at])
        to_x, to_y = after((jnp.concatenate(to_x, axis=0), jnp.concatenate(to_y, axis=0)), gate)
        return [swap(to_x, X), swap(to_y, Y)]

    def end(at, got, others):
        (from_x, from_y), others = lax.optimization_barrier((got, others))
        if at:
            stack, x, y = stacks[at - 1]
            evens[groups[at - 1][0]] = jnp.concatenate([stack[first], x[first], y[first], from_y[:tokens]], axis=1)
            evens[groups[at - 1][1]] = jnp.concatenate([stack[second], x[second], y[second], from_x[:tokens]], axis=1)
        if at < len(groups):
            stacks[at] = (stacks[at], from_x[-2 * tokens :], from_y[-2 * tokens :])
        return [from_x, from_y] + others

    found = [0, X, Y, X + Y]
    held = [basis_in_held[0], basis_out_held[0]]

    def rows_for_other(side, gate):
        return swap(in_order(after(held[side], gate), column, [CORE + i for i in found]), CORE)

    stacks, evens = {}, {}
    ours = [in_order(block, column, found) for block in held]
    theirs = [rows_for_other(0, []), None]
    gate = end(0, begin(0, []), [fetch(0, 1, []), fetch(0, 2, []), theirs[0]])

    got = begin(1, gate)
    gate = end(1, got, [fetch(0, 3, gate), fetch(1, 1, gate), fetch(1, 2, gate)])

    got = begin(2, gate)
    theirs[1] = rows_for_other(1, gate)
    half = half_product((0, 0), after(evens[0, 0], fetch(1, 3, gate)))
    gate = end(2, got, [pieces[1, 3], half, theirs[1]])

    got = begin(3, gate)
    crossed = cross(half, gate)
    even, even_1 = after([evens[0, 2], evens[0, 1]], crossed)
    rotate((0, 2), even, cross(half_product((0, 2), even), []))
    passed_in = pass_on(0)
    rotate((0, 0), evens[0, 0], crossed)
    half = half_product((0, 1), even_1)
    gate = end(3, got, [passed_in, half])

    got = begin(4, gate)
    crossed = cross(half, gate)
    rotate((0, 1), even_1, crossed)
    in_from_behind = send_ahead(0, passed_in, gate)
    even, even_2 = after([evens[0, 3], evens[1, 2]], crossed)
    rotate((0, 3), even, cross(half_product((0, 3), even), []))
    in_from_ahead = send_behind(0)
    rotate((1, 2), even_2, cross(half_product((1, 2), even_2), []))
    passed_out = pass_on(1)
    gate = end(4, got, [rotated[0, 3], rotated[1, 2]])

    rot_in = after(keep(0, in_from_behind, in_from_ahead), gate)
    for key in [(1, 1), (1, 3), (1, 0)]:
        rotate(key, evens[key], cross(half_product(key, evens[key]), []))
    all_rot_in = lax.all_gather(rot_in, "tensor", axis=1, tiled=True)
    rot_out = keep(1, send_ahead(1, passed_out, []), send_behind(1))
    return product_and_divide(rot_out, all_rot_in, eig_lambda, tokens)


def solution(mesh):
    placed = (
        P("dp", None, "tensor"),
        P("dp", None, "tensor"),
        P("dp", None, "tensor"),
        P("dp", None, "tensor"),
        P(),
        P("tensor", None),
    )
    n_dp, n_tensor = mesh.shape["dp"], mesh.shape["tensor"]

    def step(acts, *rest):
        whole = 2 * n_dp * acts.shape[1] * acts.shape[2] * n_tensor * acts.dtype.itemsize
        if whole <= ROOM and n_dp == 4 and n_tensor == X + Y + CORE + 1:
            return move_inputs(n_dp, acts, *rest)
        return move_bases(acts, *rest)

    return jax.shard_map(step, mesh=mesh, in_specs=placed, out_specs=P("dp", "tensor", None), check_vma=False)
```

```python
import jax
import jax.numpy as jnp
from jax import lax
from jax.sharding import PartitionSpec as P

damping = 0.01
ROOM = 2**25


def product_and_divide(rot_out, all_rot_in, eig_lambda, tokens):
    denom = eig_lambda.astype(jnp.float32) + damping
    contract = (((0,), (0,)), ((), ()))
    product = lax.dot_general(rot_out, all_rot_in, contract, preferred_element_type=jnp.float32) / tokens
    return (product / denom).astype(jnp.bfloat16)[None]


def from_owner(held, owner):
    return lax.psum(jnp.where(lax.axis_index("dp") == owner, held, jnp.zeros_like(held)), "dp")


def dot(a, b):
    return jnp.dot(a, b, preferred_element_type=jnp.float32)


def move_bases(acts, grads, basis_in_held, basis_out_held, owners, eig_lambda):
    column = lax.axis_index("tensor")
    basis_in = from_owner(basis_in_held[0], owners[0, column])
    basis_out = from_owner(basis_out_held[0], owners[1, column])
    rot_in = dot(lax.all_gather(acts[0], "tensor", axis=1, tiled=True), basis_in).astype(jnp.bfloat16)
    rot_out = dot(lax.all_gather(grads[0], "tensor", axis=1, tiled=True), basis_out).astype(jnp.bfloat16)
    return product_and_divide(
        rot_out, lax.all_gather(rot_in, "tensor", axis=1, tiled=True), eig_lambda, acts.shape[1]
    )


X, Y, CORE = 2, 4, 1


def swap(block, bit):
    return lax.ppermute(block, "tensor", [(j, j ^ bit) for j in range(X + Y + CORE + 1)])


def shift(block, by, n):
    return lax.ppermute(block, "dp", [(z, (z + by) % n) for z in range(n)])


def in_order(held, column, offsets):
    width = held.shape[0] // (X + Y + CORE + 1)
    blocks = [lax.dynamic_slice(held, ((column ^ i) * width, 0), (width, held.shape[1])) for i in offsets]
    return jnp.concatenate(blocks, axis=0)


def after(values, others):
    return lax.optimization_barrier((values, others))[0]


def move_inputs(n_dp, acts, grads, basis_in_held, basis_out_held, owners, eig_lambda):
    column = lax.axis_index("tensor")
    me = lax.axis_index("dp")
    own = (acts[0], grads[0])
    tokens = acts.shape[1]
    behind = [(me - owners[side, column]) % n_dp for side in (0, 1)]
    found = [0, X, Y, X + Y]
    held = (basis_in_held[0], basis_out_held[0])
    ours = [in_order(block, column, found) for block in held]

    def rows_for_other(side, gate):
        return swap(in_order(after(held[side], gate), column, [CORE + i for i in found]), CORE)

    theirs = [rows_for_other(0, []), None]

    pieces = {(0, 0): own[0], (1, 0): own[1]}
    rotated = {}

    def fetch(side, i, gate):
        block, by = {1: (own[side], -1), 2: (pieces.get((side, 1)), -1), 3: (own[side], 1)}[i]
        pieces[side, i] = shift(after(block, gate), by, n_dp)
        return pieces[side, i]

    def rotate(group, evens):
        crossing = [swap(dot(even, theirs[side]), CORE) for (side, _), even in zip(group, evens)]
        for (side, i), even, other in zip(group, evens, crossing):
            rotated[side, i] = (dot(even, ours[side]) + other).astype(jnp.bfloat16)
        return [rotated[key] for key in group]

    def pass_on(side):
        return shift(rotated[side, 2], 1, n_dp)

    def send_ahead(side, passed, gate):
        best = jnp.where(behind[side] == 0, rotated[side, 1], passed)
        return shift(after(best, gate), 1, n_dp)

    def send_behind(side):
        return shift(rotated[side, 3], -1, n_dp)

    def keep(side, from_behind, from_ahead):
        foreign = jnp.where(behind[side] == n_dp - 1, from_ahead, from_behind)
        return jnp.where(behind[side] == 0, rotated[side, 0], foreign)

    groups = [[(0, 0), (1, 0)], [(0, 1), (0, 2)], [(0, 3), (1, 2)], [(1, 1), (1, 3)]]
    first, second = slice(0, tokens), slice(tokens, 2 * tokens)

    def slot(at, gate):
        to_x, to_y = [], []
        if at:
            stack, x, y = stacks[at - 1]
            to_x.append(y[second])
            to_y.append(x[first])
        if at < len(groups):
            new = jnp.concatenate([pieces[key] for key in groups[at]], axis=0)
            to_x.append(new)
            to_y.append(new)
        to_x, to_y = after((jnp.concatenate(to_x, axis=0), jnp.concatenate(to_y, axis=0)), gate)
        got = [swap(to_x, X), swap(to_y, Y)]
        from_x, from_y = after(got, [])
        if at:
            evens[at - 1] = [
                jnp.concatenate([stack[first], x[first], y[first], from_y[:tokens]], axis=1),
                jnp.concatenate([stack[second], x[second], y[second], from_x[:tokens]], axis=1),
            ]
        if at < len(groups):
            stacks[at] = (new, from_x[-2 * tokens :], from_y[-2 * tokens :])
        return got

    stacks, evens = {}, {}
    due = slot(0, [])
    due += [fetch(0, 1, []), fetch(0, 2, []), theirs[0]]

    gate, due = due, slot(1, due)
    due += [fetch(0, 3, gate), fetch(1, 1, gate), fetch(1, 2, gate)]
    inverse = after(1 / (tokens * (eig_lambda.astype(jnp.float32) + damping)), [])
    due.append(inverse)

    gate, due = due, slot(2, due)
    theirs[1] = rows_for_other(1, gate)
    due += [fetch(1, 3, gate), theirs[1]]

    gate, due = due, slot(3, due)
    rotate(groups[1], after(evens[1], gate))
    passed_in = pass_on(0)
    due.append(passed_in)
    rotate(groups[0], after(evens[0], gate))

    gate, due = due, slot(4, due)
    in_from_behind = send_ahead(0, passed_in, gate)
    ready = rotate(groups[2], after(evens[2], gate))
    in_from_ahead = send_behind(0)
    passed_out = pass_on(1)
    ready += rotate(groups[3], after(evens[3], rotated[0, 3]))
    rot_in = after(keep(0, in_from_behind, in_from_ahead), ready)
    all_rot_in = lax.all_gather(rot_in, "tensor", axis=1, tiled=True)
    rot_out = keep(1, send_ahead(1, passed_out, []), send_behind(1))
    contract = (((0,), (0,)), ((), ()))
    product = lax.dot_general(rot_out, all_rot_in, contract, preferred_element_type=jnp.float32)
    return (product * inverse).astype(jnp.bfloat16)[None]


def solution(mesh):
    placed = (
        P("dp", None, "tensor"),
        P("dp", None, "tensor"),
        P("dp", None, "tensor"),
        P("dp", None, "tensor"),
        P(),
        P("tensor", None),
    )
    n_dp, n_tensor = mesh.shape["dp"], mesh.shape["tensor"]

    def step(acts, *rest):
        whole = 2 * n_dp * acts.shape[1] * acts.shape[2] * n_tensor * acts.dtype.itemsize
        if whole <= ROOM and n_dp == 4 and n_tensor == X + Y + CORE + 1:
            return move_inputs(n_dp, acts, *rest)
        return move_bases(acts, *rest)

    return jax.shard_map(step, mesh=mesh, in_specs=placed, out_specs=P("dp", "tensor", None), check_vma=False)
```

```python
import jax
import jax.numpy as jnp
from jax import lax
from jax.sharding import PartitionSpec as P

damping = 0.01
ROOM = 2**25


def product_and_divide(rot_out, all_rot_in, eig_lambda, tokens):
    denom = eig_lambda.astype(jnp.float32) + damping
    contract = (((0,), (0,)), ((), ()))
    product = lax.dot_general(rot_out, all_rot_in, contract, preferred_element_type=jnp.float32) / tokens
    return (product / denom).astype(jnp.bfloat16)[None]


def from_owner(held, owner):
    return lax.psum(jnp.where(lax.axis_index("dp") == owner, held, jnp.zeros_like(held)), "dp")


def dot(a, b):
    return jnp.dot(a, b, preferred_element_type=jnp.float32)


def move_bases(acts, grads, basis_in_held, basis_out_held, owners, eig_lambda):
    column = lax.axis_index("tensor")
    basis_in = from_owner(basis_in_held[0], owners[0, column])
    basis_out = from_owner(basis_out_held[0], owners[1, column])
    rot_in = dot(lax.all_gather(acts[0], "tensor", axis=1, tiled=True), basis_in).astype(jnp.bfloat16)
    rot_out = dot(lax.all_gather(grads[0], "tensor", axis=1, tiled=True), basis_out).astype(jnp.bfloat16)
    return product_and_divide(
        rot_out, lax.all_gather(rot_in, "tensor", axis=1, tiled=True), eig_lambda, acts.shape[1]
    )


X, Y, CORE = 2, 4, 1


def swap(block, bit):
    return lax.ppermute(block, "tensor", [(j, j ^ bit) for j in range(X + Y + CORE + 1)])


def shift(block, by, n):
    return lax.ppermute(block, "dp", [(z, (z + by) % n) for z in range(n)])


def in_order(held, column, offsets):
    width = held.shape[0] // (X + Y + CORE + 1)
    blocks = [lax.dynamic_slice(held, ((column ^ i) * width, 0), (width, held.shape[1])) for i in offsets]
    return jnp.concatenate(blocks, axis=0)


def after(values, others):
    return lax.optimization_barrier((values, others))[0]


def move_inputs(n_dp, acts, grads, basis_in_held, basis_out_held, owners, eig_lambda):
    column = lax.axis_index("tensor")
    me = lax.axis_index("dp")
    own = (acts[0], grads[0])
    tokens = acts.shape[1]
    behind = [(me - owners[side, column]) % n_dp for side in (0, 1)]
    found = [0, X, Y, X + Y]
    held = (basis_in_held[0], basis_out_held[0])
    ours = [in_order(block, column, found) for block in held]

    def rows_for_other(side, gate):
        return swap(in_order(after(held[side], gate), column, [CORE + i for i in found]), CORE)

    theirs = [rows_for_other(0, []), None]

    pieces = {(0, 0): own[0], (1, 0): own[1]}
    rotated, halves = {}, {}

    def fetch(side, i, gate):
        block, by = {1: (own[side], -1), 2: (pieces.get((side, 1)), -1), 3: (own[side], 1)}[i]
        pieces[side, i] = shift(after(block, gate), by, n_dp)
        return pieces[side, i]

    def rotate(group, evens):
        for (side, i), even in zip(group, evens):
            halves[side, i] = dot(even, theirs[side])
        for (side, i), even in zip(group, evens):
            rotated[side, i] = (dot(even, ours[side]) + swap(halves[side, i], CORE)).astype(jnp.bfloat16)
        return [rotated[key] for key in group]

    def pass_on(side):
        return shift(rotated[side, 2], 1, n_dp)

    def send_ahead(side, passed, gate):
        best = jnp.where(behind[side] == 0, rotated[side, 1], passed)
        return shift(after(best, gate), 1, n_dp)

    def send_behind(side):
        return shift(rotated[side, 3], -1, n_dp)

    def keep(side, from_behind, from_ahead):
        foreign = jnp.where(behind[side] == n_dp - 1, from_ahead, from_behind)
        return jnp.where(behind[side] == 0, rotated[side, 0], foreign)

    groups = [[(0, 0), (1, 0)], [(0, 1), (0, 2)], [(0, 3), (1, 2)], [(1, 1), (1, 3)]]
    first, second = slice(0, tokens), slice(tokens, 2 * tokens)

    def slot(at, gate):
        to_x, to_y = [], []
        if at:
            stack, x, y = stacks[at - 1]
            to_x.append(y[second])
            to_y.append(x[first])
        if at < len(groups):
            new = jnp.concatenate([pieces[key] for key in groups[at]], axis=0)
            to_x.append(new)
            to_y.append(new)
        to_x, to_y = after((jnp.concatenate(to_x, axis=0), jnp.concatenate(to_y, axis=0)), gate)
        got = [swap(to_x, X), swap(to_y, Y)]
        from_x, from_y = after(got, [])
        if at:
            evens[at - 1] = [
                jnp.concatenate([stack[first], x[first], y[first], from_y[:tokens]], axis=1),
                jnp.concatenate([stack[second], x[second], y[second], from_x[:tokens]], axis=1),
            ]
        if at < len(groups):
            stacks[at] = (new, from_x[-2 * tokens :], from_y[-2 * tokens :])
        return got

    stacks, evens = {}, {}
    due = slot(0, [])
    due += [fetch(0, 1, []), fetch(0, 2, []), theirs[0]]

    gate, due = due, slot(1, due)
    due += [fetch(0, 3, gate), fetch(1, 1, gate), fetch(1, 2, gate)]

    gate, due = due, slot(2, due)
    theirs[1] = rows_for_other(1, gate)
    due += [fetch(1, 3, gate), theirs[1]]

    gate, due = due, slot(3, due)
    rotate(groups[1], after(evens[1], gate))
    passed_in = pass_on(0)
    due.append(passed_in)
    rotate(groups[0], after(evens[0], gate))

    gate, due = due, slot(4, due)
    in_from_behind = send_ahead(0, passed_in, gate)
    rotate(groups[2], after(evens[2], gate))
    in_from_ahead = send_behind(0)
    passed_out = pass_on(1)
    rotate(groups[3], after(evens[3], rotated[0, 3]))
    begun = [rotated[1, 2], halves[1, 1], halves[1, 3]]
    rot_in = after(keep(0, in_from_behind, in_from_ahead), begun)
    all_rot_in = lax.all_gather(rot_in, "tensor", axis=1, tiled=True)
    rot_out = keep(1, send_ahead(1, passed_out, []), send_behind(1))
    return product_and_divide(rot_out, all_rot_in, eig_lambda, tokens)


def solution(mesh):
    placed = (
        P("dp", None, "tensor"),
        P("dp", None, "tensor"),
        P("dp", None, "tensor"),
        P("dp", None, "tensor"),
        P(),
        P("tensor", None),
    )
    n_dp, n_tensor = mesh.shape["dp"], mesh.shape["tensor"]

    def step(acts, *rest):
        whole = 2 * n_dp * acts.shape[1] * acts.shape[2] * n_tensor * acts.dtype.itemsize
        if whole <= ROOM and n_dp == 4 and n_tensor == X + Y + CORE + 1:
            return move_inputs(n_dp, acts, *rest)
        return move_bases(acts, *rest)

    return jax.shard_map(step, mesh=mesh, in_specs=placed, out_specs=P("dp", "tensor", None), check_vma=False)
```

```python
import jax
import jax.numpy as jnp
from jax import lax
from jax.sharding import PartitionSpec as P

damping = 0.01
ROOM = 2**25


def product_and_divide(rot_out, all_rot_in, eig_lambda, tokens):
    denom = eig_lambda.astype(jnp.float32) + damping
    contract = (((0,), (0,)), ((), ()))
    product = lax.dot_general(rot_out, all_rot_in, contract, preferred_element_type=jnp.float32) / tokens
    return (product / denom).astype(jnp.bfloat16)[None]


def from_owner(held, owner):
    return lax.psum(jnp.where(lax.axis_index("dp") == owner, held, jnp.zeros_like(held)), "dp")


def dot(a, b):
    return jnp.dot(a, b, preferred_element_type=jnp.float32)


def move_bases(acts, grads, basis_in_held, basis_out_held, owners, eig_lambda):
    column = lax.axis_index("tensor")
    basis_in = from_owner(basis_in_held[0], owners[0, column])
    basis_out = from_owner(basis_out_held[0], owners[1, column])
    rot_in = dot(lax.all_gather(acts[0], "tensor", axis=1, tiled=True), basis_in).astype(jnp.bfloat16)
    rot_out = dot(lax.all_gather(grads[0], "tensor", axis=1, tiled=True), basis_out).astype(jnp.bfloat16)
    return product_and_divide(
        rot_out, lax.all_gather(rot_in, "tensor", axis=1, tiled=True), eig_lambda, acts.shape[1]
    )


X, Y, CORE = 2, 4, 1


def swap(block, bit):
    return lax.ppermute(block, "tensor", [(j, j ^ bit) for j in range(X + Y + CORE + 1)])


def shift(block, by, n):
    return lax.ppermute(block, "dp", [(z, (z + by) % n) for z in range(n)])


def in_order(held, column, offsets):
    width = held.shape[0] // (X + Y + CORE + 1)
    blocks = [lax.dynamic_slice(held, ((column ^ i) * width, 0), (width, held.shape[1])) for i in offsets]
    return jnp.concatenate(blocks, axis=0)


def after(values, others):
    return lax.optimization_barrier((values, others))[0]


def move_inputs(n_dp, acts, grads, basis_in_held, basis_out_held, owners, eig_lambda):
    column = lax.axis_index("tensor")
    me = lax.axis_index("dp")
    own = (acts[0], grads[0])
    tokens = acts.shape[1]
    behind = [(me - owners[side, column]) % n_dp for side in (0, 1)]
    found = [0, X, Y, X + Y]
    held = (basis_in_held[0], basis_out_held[0])
    ours = [in_order(block, column, found) for block in held]

    def rows_for_other(side, gate):
        return swap(in_order(after(held[side], gate), column, [CORE + i for i in found]), CORE)

    theirs = [rows_for_other(0, []), None]

    pieces = {(0, 0): own[0], (1, 0): own[1]}
    rotated, halves = {}, {}

    def fetch(side, i, gate):
        block, by = {1: (own[side], -1), 2: (pieces.get((side, 1)), -1), 3: (own[side], 1)}[i]
        pieces[side, i] = shift(after(block, gate), by, n_dp)
        return pieces[side, i]

    def rotate(group, evens):
        for (side, i), even in zip(group, evens):
            halves[side, i] = dot(even, theirs[side])
        for (side, i), even in zip(group, evens):
            rotated[side, i] = (dot(even, ours[side]) + swap(halves[side, i], CORE)).astype(jnp.bfloat16)
        return [rotated[key] for key in group]

    def pass_on(side):
        return shift(rotated[side, 2], 1, n_dp)

    def send_ahead(side, passed, gate):
        best = jnp.where(behind[side] == 0, rotated[side, 1], passed)
        return shift(after(best, gate), 1, n_dp)

    def send_behind(side):
        return shift(rotated[side, 3], -1, n_dp)

    def keep(side, from_behind, from_ahead):
        foreign = jnp.where(behind[side] == n_dp - 1, from_ahead, from_behind)
        return jnp.where(behind[side] == 0, rotated[side, 0], foreign)

    groups = [[(0, 0), (1, 0)], [(0, 1), (0, 2)], [(0, 3), (1, 2)], [(1, 1), (1, 3)]]
    first, second = slice(0, tokens), slice(tokens, 2 * tokens)

    def slot(at, gate):
        to_x, to_y = [], []
        if at:
            _, x, y = stacks[at - 1]
            to_x.append(y[second])
            to_y.append(x[first])
        if at < len(groups):
            stacks[at] = jnp.concatenate([pieces[key] for key in groups[at]], axis=0)
            to_x.append(stacks[at])
            to_y.append(stacks[at])
        to_x, to_y = after((jnp.concatenate(to_x, axis=0), jnp.concatenate(to_y, axis=0)), gate)
        return [swap(to_x, X), swap(to_y, Y)]

    def use(at, got, others):
        from_x, from_y = after(got, others)
        if at:
            stack, x, y = stacks[at - 1]
            evens[at - 1] = [
                jnp.concatenate([stack[first], x[first], y[first], from_y[:tokens]], axis=1),
                jnp.concatenate([stack[second], x[second], y[second], from_x[:tokens]], axis=1),
            ]
        if at < len(groups):
            stacks[at] = (stacks[at], from_x[-2 * tokens :], from_y[-2 * tokens :])

    stacks, evens = {}, {}
    due = slot(0, [])
    use(0, due, [])
    due += [fetch(0, 1, []), fetch(0, 2, []), theirs[0]]

    gate, due = due, slot(1, due)
    use(1, due, [])
    due += [fetch(0, 3, gate), fetch(1, 1, gate), fetch(1, 2, gate)]

    gate, due = due, slot(2, due)
    use(2, due, [])
    theirs[1] = rows_for_other(1, gate)
    due += [fetch(1, 3, gate), theirs[1]]

    gate, due = due, slot(3, due)
    use(3, due, [])
    rotate(groups[1], after(evens[1], gate))
    passed_in = pass_on(0)
    due.append(passed_in)
    rotate(groups[0][:1], after(evens[0][:1], gate))

    gate, due = due, slot(4, due)
    in_from_behind = send_ahead(0, passed_in, gate)
    rotate(groups[2], after(evens[2], gate))
    in_from_ahead = send_behind(0)
    passed_out = pass_on(1)
    rotate(groups[0][1:], after(evens[0][1:], passed_out))
    use(4, due, rotated[0, 3])
    rotate(groups[3], evens[3])
    begun = [rotated[1, 2], halves[1, 1], halves[1, 3]]
    rot_in = after(keep(0, in_from_behind, in_from_ahead), begun)
    all_rot_in = lax.all_gather(rot_in, "tensor", axis=1, tiled=True)
    rot_out = keep(1, send_ahead(1, passed_out, []), send_behind(1))
    return product_and_divide(rot_out, all_rot_in, eig_lambda, tokens)


def solution(mesh):
    placed = (
        P("dp", None, "tensor"),
        P("dp", None, "tensor"),
        P("dp", None, "tensor"),
        P("dp", None, "tensor"),
        P(),
        P("tensor", None),
    )
    n_dp, n_tensor = mesh.shape["dp"], mesh.shape["tensor"]

    def step(acts, *rest):
        whole = 2 * n_dp * acts.shape[1] * acts.shape[2] * n_tensor * acts.dtype.itemsize
        if whole <= ROOM and n_dp == 4 and n_tensor == X + Y + CORE + 1:
            return move_inputs(n_dp, acts, *rest)
        return move_bases(acts, *rest)

    return jax.shard_map(step, mesh=mesh, in_specs=placed, out_specs=P("dp", "tensor", None), check_vma=False)
```

```python
import jax
import jax.numpy as jnp
from jax import lax
from jax.sharding import PartitionSpec as P

damping = 0.01
ROOM = 2**25


def product_and_divide(rot_out, all_rot_in, eig_lambda, tokens):
    denom = eig_lambda.astype(jnp.float32) + damping
    contract = (((0,), (0,)), ((), ()))
    product = lax.dot_general(rot_out, all_rot_in, contract, preferred_element_type=jnp.float32) / tokens
    return (product / denom).astype(jnp.bfloat16)[None]


def from_owner(held, owner):
    return lax.psum(jnp.where(lax.axis_index("dp") == owner, held, jnp.zeros_like(held)), "dp")


def dot(a, b):
    return jnp.dot(a, b, preferred_element_type=jnp.float32)


def move_bases(acts, grads, basis_in_held, basis_out_held, owners, eig_lambda):
    column = lax.axis_index("tensor")
    basis_in = from_owner(basis_in_held[0], owners[0, column])
    basis_out = from_owner(basis_out_held[0], owners[1, column])
    rot_in = dot(lax.all_gather(acts[0], "tensor", axis=1, tiled=True), basis_in).astype(jnp.bfloat16)
    rot_out = dot(lax.all_gather(grads[0], "tensor", axis=1, tiled=True), basis_out).astype(jnp.bfloat16)
    return product_and_divide(
        rot_out, lax.all_gather(rot_in, "tensor", axis=1, tiled=True), eig_lambda, acts.shape[1]
    )


X, Y, CORE = 2, 4, 1


def swap(block, bit):
    return lax.ppermute(block, "tensor", [(j, j ^ bit) for j in range(X + Y + CORE + 1)])


def shift(block, by, n):
    return lax.ppermute(block, "dp", [(z, (z + by) % n) for z in range(n)])


def in_order(held, column, offsets):
    width = held.shape[0] // (X + Y + CORE + 1)
    blocks = [lax.dynamic_slice(held, ((column ^ i) * width, 0), (width, held.shape[1])) for i in offsets]
    return jnp.concatenate(blocks, axis=0)


def after(values, others):
    return lax.optimization_barrier((values, others))[0]


def move_inputs(n_dp, acts, grads, basis_in_held, basis_out_held, owners, eig_lambda):
    column = lax.axis_index("tensor")
    me = lax.axis_index("dp")
    own = (acts[0], grads[0])
    tokens = acts.shape[1]
    behind = [(me - owners[side, column]) % n_dp for side in (0, 1)]
    found = [0, X, Y, X + Y]
    held = (basis_in_held[0], basis_out_held[0])
    ours = [in_order(block, column, found) for block in held]

    def rows_for_other(side, gate):
        return swap(in_order(after(held[side], gate), column, [CORE + i for i in found]), CORE)

    theirs = [rows_for_other(0, []), None]

    pieces = {(0, 0): own[0], (1, 0): own[1]}
    rotated, halves = {}, {}

    def fetch(side, i, gate):
        block, by = {1: (own[side], -1), 2: (pieces.get((side, 1)), -1), 3: (own[side], 1)}[i]
        pieces[side, i] = shift(after(block, gate), by, n_dp)
        return pieces[side, i]

    def rotate(group, evens):
        for (side, i), even in zip(group, evens):
            halves[side, i] = dot(even, theirs[side])
        for (side, i), even in zip(group, evens):
            rotated[side, i] = (dot(even, ours[side]) + swap(halves[side, i], CORE)).astype(jnp.bfloat16)
        return [rotated[key] for key in group]

    def pass_on(side):
        return shift(rotated[side, 2], 1, n_dp)

    def send_ahead(side, passed, gate):
        best = jnp.where(behind[side] == 0, rotated[side, 1], passed)
        return shift(after(best, gate), 1, n_dp)

    def send_behind(side):
        return shift(rotated[side, 3], -1, n_dp)

    def keep(side, from_behind, from_ahead):
        foreign = jnp.where(behind[side] == n_dp - 1, from_ahead, from_behind)
        return jnp.where(behind[side] == 0, rotated[side, 0], foreign)

    groups = [[(0, 0), (1, 0)], [(0, 1), (0, 2)], [(0, 3), (1, 2)], [(1, 1), (1, 3)]]
    first, second = slice(0, tokens), slice(tokens, 2 * tokens)

    def slot(at, gate):
        to_x, to_y = [], []
        if at:
            _, x, y = stacks[at - 1]
            to_x.append(y[second])
            to_y.append(x[first])
        if at < len(groups):
            stacks[at] = jnp.concatenate([pieces[key] for key in groups[at]], axis=0)
            to_x.append(stacks[at])
            to_y.append(stacks[at])
        to_x, to_y = after((jnp.concatenate(to_x, axis=0), jnp.concatenate(to_y, axis=0)), gate)
        return [swap(to_x, X), swap(to_y, Y)]

    def use(at, got, others):
        from_x, from_y = after(got, others)
        if at:
            stack, x, y = stacks[at - 1]
            evens[at - 1] = [
                jnp.concatenate([stack[first], x[first], y[first], from_y[:tokens]], axis=1),
                jnp.concatenate([stack[second], x[second], y[second], from_x[:tokens]], axis=1),
            ]
        if at < len(groups):
            stacks[at] = (stacks[at], from_x[-2 * tokens :], from_y[-2 * tokens :])

    stacks, evens = {}, {}
    due = slot(0, [])
    use(0, due, [])
    due += [fetch(0, 1, []), fetch(0, 2, []), theirs[0]]

    gate, due = due, slot(1, due)
    use(1, due, [])
    due += [fetch(0, 3, gate), fetch(1, 1, gate), fetch(1, 2, gate)]

    gate, due = due, slot(2, due)
    use(2, due, [])
    theirs[1] = rows_for_other(1, gate)
    due += [fetch(1, 3, gate), theirs[1]] + rotate(groups[0][:1], evens[0][:1])

    gate, due = due, slot(3, due)
    use(3, due, [])
    rotate(groups[1], after(evens[1], gate))
    passed_in = pass_on(0)
    due += [passed_in] + rotate(groups[0][1:], after(evens[0][1:], gate))

    gate, due = due, slot(4, due)
    in_from_behind = send_ahead(0, passed_in, gate)
    rotate(groups[2], after(evens[2], gate))
    in_from_ahead = send_behind(0)
    passed_out = pass_on(1)
    use(4, due, rotated[0, 3])
    rotate(groups[3], evens[3])
    begun = [rotated[1, 2], halves[1, 1], halves[1, 3]]
    rot_in = after(keep(0, in_from_behind, in_from_ahead), begun)
    all_rot_in = lax.all_gather(rot_in, "tensor", axis=1, tiled=True)
    rot_out = keep(1, send_ahead(1, passed_out, []), send_behind(1))
    return product_and_divide(rot_out, all_rot_in, eig_lambda, tokens)


def solution(mesh):
    placed = (
        P("dp", None, "tensor"),
        P("dp", None, "tensor"),
        P("dp", None, "tensor"),
        P("dp", None, "tensor"),
        P(),
        P("tensor", None),
    )
    n_dp, n_tensor = mesh.shape["dp"], mesh.shape["tensor"]

    def step(acts, *rest):
        whole = 2 * n_dp * acts.shape[1] * acts.shape[2] * n_tensor * acts.dtype.itemsize
        if whole <= ROOM and n_dp == 4 and n_tensor == X + Y + CORE + 1:
            return move_inputs(n_dp, acts, *rest)
        return move_bases(acts, *rest)

    return jax.shard_map(step, mesh=mesh, in_specs=placed, out_specs=P("dp", "tensor", None), check_vma=False)
```

```python
import jax
import jax.numpy as jnp
from jax import lax
from jax.sharding import PartitionSpec as P

damping = 0.01
ROOM = 2**25


def product_and_divide(rot_out, all_rot_in, eig_lambda, tokens):
    denom = eig_lambda.astype(jnp.float32) + damping
    contract = (((0,), (0,)), ((), ()))
    product = lax.dot_general(rot_out, all_rot_in, contract, preferred_element_type=jnp.float32) / tokens
    return (product / denom).astype(jnp.bfloat16)[None]


def from_owner(held, owner):
    return lax.psum(jnp.where(lax.axis_index("dp") == owner, held, jnp.zeros_like(held)), "dp")


def dot(a, b):
    return jnp.dot(a, b, preferred_element_type=jnp.float32)


def move_bases(acts, grads, basis_in_held, basis_out_held, owners, eig_lambda):
    column = lax.axis_index("tensor")
    basis_in = from_owner(basis_in_held[0], owners[0, column])
    basis_out = from_owner(basis_out_held[0], owners[1, column])
    rot_in = dot(lax.all_gather(acts[0], "tensor", axis=1, tiled=True), basis_in).astype(jnp.bfloat16)
    rot_out = dot(lax.all_gather(grads[0], "tensor", axis=1, tiled=True), basis_out).astype(jnp.bfloat16)
    return product_and_divide(
        rot_out, lax.all_gather(rot_in, "tensor", axis=1, tiled=True), eig_lambda, acts.shape[1]
    )


X, Y, CORE = 2, 4, 1


def swap(block, bit):
    return lax.ppermute(block, "tensor", [(j, j ^ bit) for j in range(X + Y + CORE + 1)])


def shift(block, by, n):
    return lax.ppermute(block, "dp", [(z, (z + by) % n) for z in range(n)])


def in_order(held, column, offsets):
    width = held.shape[0] // (X + Y + CORE + 1)
    blocks = [lax.dynamic_slice(held, ((column ^ i) * width, 0), (width, held.shape[1])) for i in offsets]
    return jnp.concatenate(blocks, axis=0)


def after(values, others):
    return lax.optimization_barrier((values, others))[0]


def move_inputs(n_dp, acts, grads, basis_in_held, basis_out_held, owners, eig_lambda):
    column = lax.axis_index("tensor")
    me = lax.axis_index("dp")
    own = (acts[0], grads[0])
    tokens = acts.shape[1]
    behind = [(me - owners[side, column]) % n_dp for side in (0, 1)]
    found = [0, X, Y, X + Y]
    held = (basis_in_held[0], basis_out_held[0])
    ours = [in_order(block, column, found) for block in held]

    def rows_for_other(side, gate):
        return swap(in_order(after(held[side], gate), column, [CORE + i for i in found]), CORE)

    theirs = [rows_for_other(0, []), None]

    pieces = {(0, 0): own[0], (1, 0): own[1]}
    rotated, halves = {}, {}

    def fetch(side, i, gate):
        block, by = {1: (own[side], -1), 2: (pieces.get((side, 1)), -1), 3: (own[side], 1)}[i]
        pieces[side, i] = shift(after(block, gate), by, n_dp)
        return pieces[side, i]

    def rotate(group, evens):
        for (side, i), even in zip(group, evens):
            halves[side, i] = dot(even, theirs[side])
        for (side, i), even in zip(group, evens):
            rotated[side, i] = (dot(even, ours[side]) + swap(halves[side, i], CORE)).astype(jnp.bfloat16)
        return [rotated[key] for key in group]

    def pass_on(side):
        return shift(rotated[side, 2], 1, n_dp)

    def send_ahead(side, passed, gate):
        best = jnp.where(behind[side] == 0, rotated[side, 1], passed)
        return shift(after(best, gate), 1, n_dp)

    def send_behind(side):
        return shift(rotated[side, 3], -1, n_dp)

    def keep(side, from_behind, from_ahead):
        foreign = jnp.where(behind[side] == n_dp - 1, from_ahead, from_behind)
        return jnp.where(behind[side] == 0, rotated[side, 0], foreign)

    groups = [[(0, 0), (1, 0)], [(0, 1), (0, 2)], [(0, 3), (1, 2)], [(1, 1), (1, 3)]]
    first, second = slice(0, tokens), slice(tokens, 2 * tokens)

    def slot(at, gate):
        to_x, to_y = [], []
        if at:
            stack, x, y = stacks[at - 1]
            to_x.append(y[second])
            to_y.append(x[first])
        if at < len(groups):
            new = jnp.concatenate([pieces[key] for key in groups[at]], axis=0)
            to_x.append(new)
            to_y.append(new)
        to_x, to_y = after((jnp.concatenate(to_x, axis=0), jnp.concatenate(to_y, axis=0)), gate)
        got = [swap(to_x, X), swap(to_y, Y)]
        from_x, from_y = after(got, [])
        if at:
            evens[at - 1] = [
                jnp.concatenate([stack[first], x[first], y[first], from_y[:tokens]], axis=1),
                jnp.concatenate([stack[second], x[second], y[second], from_x[:tokens]], axis=1),
            ]
        if at < len(groups):
            stacks[at] = (new, from_x[-2 * tokens :], from_y[-2 * tokens :])
        return got

    stacks, evens = {}, {}
    due = slot(0, [])
    due += [fetch(0, 1, []), fetch(0, 2, []), theirs[0]]

    gate, due = due, slot(1, due)
    due += [fetch(0, 3, gate), fetch(1, 1, gate), fetch(1, 2, gate)]

    gate, due = due, slot(2, due)
    theirs[1] = rows_for_other(1, gate)
    due += [fetch(1, 3, gate), theirs[1]]

    gate, due = due, slot(3, due)
    rotate(groups[1], after(evens[1], gate))
    passed_in = pass_on(0)
    due += [passed_in] + rotate(groups[0][:1], after(evens[0][:1], gate))

    gate, due = due, slot(4, due)
    in_from_behind = send_ahead(0, passed_in, gate)
    rotate(groups[2], after(evens[2], gate))
    in_from_ahead = send_behind(0)
    passed_out = pass_on(1)
    rotate(groups[3], after(evens[3], rotated[0, 3]))
    begun = [rotated[1, 2], halves[1, 1], halves[1, 3]]
    rot_in = after(keep(0, in_from_behind, in_from_ahead), begun)
    all_rot_in = lax.all_gather(rot_in, "tensor", axis=1, tiled=True)
    rotate(groups[0][1:], after(evens[0][1:], [rotated[1, 1], rotated[1, 3]]))
    rotated[1, 0] = after(rotated[1, 0], [])
    rot_out = keep(1, send_ahead(1, passed_out, []), send_behind(1))
    return product_and_divide(rot_out, all_rot_in, eig_lambda, tokens)


def solution(mesh):
    placed = (
        P("dp", None, "tensor"),
        P("dp", None, "tensor"),
        P("dp", None, "tensor"),
        P("dp", None, "tensor"),
        P(),
        P("tensor", None),
    )
    n_dp, n_tensor = mesh.shape["dp"], mesh.shape["tensor"]

    def step(acts, *rest):
        whole = 2 * n_dp * acts.shape[1] * acts.shape[2] * n_tensor * acts.dtype.itemsize
        if whole <= ROOM and n_dp == 4 and n_tensor == X + Y + CORE + 1:
            return move_inputs(n_dp, acts, *rest)
        return move_bases(acts, *rest)

    return jax.shard_map(step, mesh=mesh, in_specs=placed, out_specs=P("dp", "tensor", None), check_vma=False)
```

```python
import jax
import jax.numpy as jnp
from jax import lax
from jax.sharding import PartitionSpec as P

damping = 0.01
ROOM = 2**25


def product_and_divide(rot_out, all_rot_in, eig_lambda, tokens):
    denom = eig_lambda.astype(jnp.float32) + damping
    contract = (((0,), (0,)), ((), ()))
    product = lax.dot_general(rot_out, all_rot_in, contract, preferred_element_type=jnp.float32) / tokens
    return (product / denom).astype(jnp.bfloat16)[None]


def from_owner(held, owner):
    return lax.psum(jnp.where(lax.axis_index("dp") == owner, held, jnp.zeros_like(held)), "dp")


def dot(a, b):
    return jnp.dot(a, b, preferred_element_type=jnp.float32)


def move_bases(acts, grads, basis_in_held, basis_out_held, owners, eig_lambda):
    column = lax.axis_index("tensor")
    basis_in = from_owner(basis_in_held[0], owners[0, column])
    basis_out = from_owner(basis_out_held[0], owners[1, column])
    rot_in = dot(lax.all_gather(acts[0], "tensor", axis=1, tiled=True), basis_in).astype(jnp.bfloat16)
    rot_out = dot(lax.all_gather(grads[0], "tensor", axis=1, tiled=True), basis_out).astype(jnp.bfloat16)
    return product_and_divide(
        rot_out, lax.all_gather(rot_in, "tensor", axis=1, tiled=True), eig_lambda, acts.shape[1]
    )


X, Y, CORE = 2, 4, 1


def swap(block, bit):
    return lax.ppermute(block, "tensor", [(j, j ^ bit) for j in range(X + Y + CORE + 1)])


def shift(block, by, n):
    return lax.ppermute(block, "dp", [(z, (z + by) % n) for z in range(n)])


def in_order(held, column, offsets):
    width = held.shape[0] // (X + Y + CORE + 1)
    blocks = [lax.dynamic_slice(held, ((column ^ i) * width, 0), (width, held.shape[1])) for i in offsets]
    return jnp.concatenate(blocks, axis=0)


def after(values, others):
    return lax.optimization_barrier((values, others))[0]


def move_inputs(n_dp, acts, grads, basis_in_held, basis_out_held, owners, eig_lambda):
    column = lax.axis_index("tensor")
    me = lax.axis_index("dp")
    own = (acts[0], grads[0])
    tokens = acts.shape[1]
    behind = [(me - owners[side, column]) % n_dp for side in (0, 1)]
    found = [0, X, Y, X + Y]
    held = (basis_in_held[0], basis_out_held[0])
    ours = [in_order(block, column, found) for block in held]

    def rows_for_other(side, gate):
        return swap(in_order(after(held[side], gate), column, [CORE + i for i in found]), CORE)

    theirs = [rows_for_other(0, []), None]

    pieces = {(0, 0): own[0], (1, 0): own[1]}
    rotated, halves = {}, {}

    def fetch(side, i, gate):
        block, by = {1: (own[side], -1), 2: (pieces.get((side, 1)), -1), 3: (own[side], 1)}[i]
        pieces[side, i] = shift(after(block, gate), by, n_dp)
        return pieces[side, i]

    def rotate(group, evens):
        for (side, i), even in zip(group, evens):
            halves[side, i] = dot(even, theirs[side])
        for (side, i), even in zip(group, evens):
            rotated[side, i] = (dot(even, ours[side]) + swap(halves[side, i], CORE)).astype(jnp.bfloat16)
        return [rotated[key] for key in group]

    def pass_on(side):
        return shift(rotated[side, 2], 1, n_dp)

    def send_ahead(side, passed, gate):
        best = jnp.where(behind[side] == 0, rotated[side, 1], passed)
        return shift(after(best, gate), 1, n_dp)

    def send_behind(side):
        return shift(rotated[side, 3], -1, n_dp)

    def keep(side, from_behind, from_ahead):
        foreign = jnp.where(behind[side] == n_dp - 1, from_ahead, from_behind)
        return jnp.where(behind[side] == 0, rotated[side, 0], foreign)

    groups = [[(0, 0), (1, 0)], [(0, 1), (0, 2)], [(0, 3), (1, 2)], [(1, 1), (1, 3)]]
    first, second = slice(0, tokens), slice(tokens, 2 * tokens)

    def slot(at, gate):
        to_x, to_y = [], []
        if at:
            _, x, y = stacks[at - 1]
            to_x.append(y[second])
            to_y.append(x[first])
        if at < len(groups):
            stacks[at] = jnp.concatenate([pieces[key] for key in groups[at]], axis=0)
            to_x.append(stacks[at])
            to_y.append(stacks[at])
        to_x, to_y = after((jnp.concatenate(to_x, axis=0), jnp.concatenate(to_y, axis=0)), gate)
        return [swap(to_x, X), swap(to_y, Y)]

    def use(at, got, others):
        from_x, from_y = after(got, others)
        if at:
            stack, x, y = stacks[at - 1]
            evens[at - 1] = [
                jnp.concatenate([stack[first], x[first], y[first], from_y[:tokens]], axis=1),
                jnp.concatenate([stack[second], x[second], y[second], from_x[:tokens]], axis=1),
            ]
        if at < len(groups):
            stacks[at] = (stacks[at], from_x[-2 * tokens :], from_y[-2 * tokens :])

    stacks, evens = {}, {}
    due = slot(0, [])
    use(0, due, [])
    due += [fetch(0, 1, []), fetch(0, 2, []), theirs[0]]

    gate, due = due, slot(1, due)
    use(1, due, [])
    due += [fetch(0, 3, gate), fetch(1, 1, gate), fetch(1, 2, gate)]

    gate, due = due, slot(2, due)
    use(2, due, [])
    theirs[1] = rows_for_other(1, gate)
    due += [fetch(1, 3, gate), theirs[1]]

    gate, due = due, slot(3, due)
    use(3, due, [])
    rotate(groups[1], after(evens[1], gate))
    passed_in = pass_on(0)
    due += [passed_in] + rotate(groups[0][:1], after(evens[0][:1], gate))

    gate, due = due, slot(4, due)
    in_from_behind = send_ahead(0, passed_in, gate)
    rotate(groups[2][:1], after(evens[2][:1], gate))
    in_from_ahead = send_behind(0)
    rotate(groups[2][1:], after(evens[2][1:], rotated[0, 3]))
    passed_out = pass_on(1)
    use(4, due, rotated[0, 3])
    rotate(groups[3], evens[3])
    begun = [rotated[1, 2], halves[1, 1], halves[1, 3]]
    rot_in = after(keep(0, in_from_behind, in_from_ahead), begun)
    all_rot_in = lax.all_gather(rot_in, "tensor", axis=1, tiled=True)
    rotate(groups[0][1:], after(evens[0][1:], [rotated[1, 1], rotated[1, 3]]))
    rotated[1, 0] = after(rotated[1, 0], [])
    rot_out = keep(1, send_ahead(1, passed_out, []), send_behind(1))
    return product_and_divide(rot_out, all_rot_in, eig_lambda, tokens)


def solution(mesh):
    placed = (
        P("dp", None, "tensor"),
        P("dp", None, "tensor"),
        P("dp", None, "tensor"),
        P("dp", None, "tensor"),
        P(),
        P("tensor", None),
    )
    n_dp, n_tensor = mesh.shape["dp"], mesh.shape["tensor"]

    def step(acts, *rest):
        whole = 2 * n_dp * acts.shape[1] * acts.shape[2] * n_tensor * acts.dtype.itemsize
        if whole <= ROOM and n_dp == 4 and n_tensor == X + Y + CORE + 1:
            return move_inputs(n_dp, acts, *rest)
        return move_bases(acts, *rest)

    return jax.shard_map(step, mesh=mesh, in_specs=placed, out_specs=P("dp", "tensor", None), check_vma=False)
```

```python
import jax
import jax.numpy as jnp
from jax import lax
from jax.sharding import PartitionSpec as P

damping = 0.01
ROOM = 2**25


def product_and_divide(rot_out, all_rot_in, eig_lambda, tokens):
    denom = eig_lambda.astype(jnp.float32) + damping
    contract = (((0,), (0,)), ((), ()))
    product = lax.dot_general(rot_out, all_rot_in, contract, preferred_element_type=jnp.float32) / tokens
    return (product / denom).astype(jnp.bfloat16)[None]


def from_owner(held, owner):
    return lax.psum(jnp.where(lax.axis_index("dp") == owner, held, jnp.zeros_like(held)), "dp")


def dot(a, b):
    return jnp.dot(a, b, preferred_element_type=jnp.float32)


def move_bases(acts, grads, basis_in_held, basis_out_held, owners, eig_lambda):
    column = lax.axis_index("tensor")
    basis_in = from_owner(basis_in_held[0], owners[0, column])
    basis_out = from_owner(basis_out_held[0], owners[1, column])
    rot_in = dot(lax.all_gather(acts[0], "tensor", axis=1, tiled=True), basis_in).astype(jnp.bfloat16)
    rot_out = dot(lax.all_gather(grads[0], "tensor", axis=1, tiled=True), basis_out).astype(jnp.bfloat16)
    return product_and_divide(
        rot_out, lax.all_gather(rot_in, "tensor", axis=1, tiled=True), eig_lambda, acts.shape[1]
    )


X, Y, CORE = 2, 4, 1


def swap(block, bit):
    return lax.ppermute(block, "tensor", [(j, j ^ bit) for j in range(X + Y + CORE + 1)])


def shift(block, by, n):
    return lax.ppermute(block, "dp", [(z, (z + by) % n) for z in range(n)])


def in_order(held, column, offsets):
    width = held.shape[0] // (X + Y + CORE + 1)
    blocks = [lax.dynamic_slice(held, ((column ^ i) * width, 0), (width, held.shape[1])) for i in offsets]
    return jnp.concatenate(blocks, axis=0)


def after(values, others):
    return lax.optimization_barrier((values, others))[0]


def move_inputs(n_dp, acts, grads, basis_in_held, basis_out_held, owners, eig_lambda):
    column = lax.axis_index("tensor")
    me = lax.axis_index("dp")
    own = (acts[0], grads[0])
    tokens = acts.shape[1]
    behind = [(me - owners[side, column]) % n_dp for side in (0, 1)]
    found = [0, X, Y, X + Y]
    held = (basis_in_held[0], basis_out_held[0])
    ours = [in_order(block, column, found) for block in held]

    def rows_for_other(side, gate):
        return swap(in_order(after(held[side], gate), column, [CORE + i for i in found]), CORE)

    theirs = [rows_for_other(0, []), None]

    pieces = {(0, 0): own[0], (1, 0): own[1]}
    rotated, halves = {}, {}

    def fetch(side, i, gate):
        block, by = {1: (own[side], -1), 2: (pieces.get((side, 1)), -1), 3: (own[side], 1)}[i]
        pieces[side, i] = shift(after(block, gate), by, n_dp)
        return pieces[side, i]

    def rotate(group, evens):
        for (side, i), even in zip(group, evens):
            halves[side, i] = dot(even, theirs[side])
        for (side, i), even in zip(group, evens):
            rotated[side, i] = (dot(even, ours[side]) + swap(halves[side, i], CORE)).astype(jnp.bfloat16)
        return [rotated[key] for key in group]

    def pass_on(side):
        return shift(rotated[side, 2], 1, n_dp)

    def send_ahead(side, passed, gate):
        best = jnp.where(behind[side] == 0, rotated[side, 1], passed)
        return shift(after(best, gate), 1, n_dp)

    def send_behind(side):
        return shift(rotated[side, 3], -1, n_dp)

    def keep(side, from_behind, from_ahead):
        foreign = jnp.where(behind[side] == n_dp - 1, from_ahead, from_behind)
        return jnp.where(behind[side] == 0, rotated[side, 0], foreign)

    groups = [[(0, 0), (1, 0)], [(0, 1), (0, 2)], [(0, 3), (1, 2)], [(1, 1), (1, 3)]]
    first, second = slice(0, tokens), slice(tokens, 2 * tokens)

    def slot(at, gate):
        to_x, to_y = [], []
        if at:
            stack, x, y = stacks[at - 1]
            to_x.append(y[second])
            to_y.append(x[first])
        if at < len(groups):
            new = jnp.concatenate([pieces[key] for key in groups[at]], axis=0)
            to_x.append(new)
            to_y.append(new)
        to_x, to_y = after((jnp.concatenate(to_x, axis=0), jnp.concatenate(to_y, axis=0)), gate)
        got = [swap(to_x, X), swap(to_y, Y)]
        from_x, from_y = after(got, [])
        if at:
            evens[at - 1] = [
                jnp.concatenate([stack[first], x[first], y[first], from_y[:tokens]], axis=1),
                jnp.concatenate([stack[second], x[second], y[second], from_x[:tokens]], axis=1),
            ]
        if at < len(groups):
            stacks[at] = (new, from_x[-2 * tokens :], from_y[-2 * tokens :])
        return got

    stacks, evens = {}, {}
    due = slot(0, [])
    due += [fetch(0, 1, []), fetch(0, 2, []), theirs[0]]

    gate, due = due, slot(1, due)
    due += [fetch(0, 3, gate), fetch(1, 1, gate), fetch(1, 2, gate)]

    gate, due = due, slot(2, due)
    theirs[1] = rows_for_other(1, gate)
    due += [fetch(1, 3, gate), theirs[1]]

    gate, due = due, slot(3, due)
    rotate(groups[1], after(evens[1], gate))
    passed_in = pass_on(0)
    due += [passed_in] + rotate(groups[0], after(evens[0], gate))

    gate, due = due, slot(4, due)
    in_from_behind = send_ahead(0, passed_in, gate)
    rotate(groups[2], after(evens[2], gate))
    in_from_ahead = send_behind(0)
    passed_out = pass_on(1)
    rotate(groups[3], after(evens[3], rotated[0, 3]))
    begun = [rotated[1, 2], halves[1, 1], halves[1, 3]]
    rot_in = after(keep(0, in_from_behind, in_from_ahead), begun)
    all_rot_in = lax.all_gather(rot_in, "tensor", axis=1, tiled=True)
    rot_out = keep(1, send_ahead(1, passed_out, []), send_behind(1))
    return product_and_divide(rot_out, all_rot_in, eig_lambda, tokens)


def solution(mesh):
    placed = (
        P("dp", None, "tensor"),
        P("dp", None, "tensor"),
        P("dp", None, "tensor"),
        P("dp", None, "tensor"),
        P(),
        P("tensor", None),
    )
    n_dp, n_tensor = mesh.shape["dp"], mesh.shape["tensor"]

    def step(acts, *rest):
        whole = 2 * n_dp * acts.shape[1] * acts.shape[2] * n_tensor * acts.dtype.itemsize
        if whole <= ROOM and n_dp == 4 and n_tensor == X + Y + CORE + 1:
            return move_inputs(n_dp, acts, *rest)
        return move_bases(acts, *rest)

    return jax.shard_map(step, mesh=mesh, in_specs=placed, out_specs=P("dp", "tensor", None), check_vma=False)
```
